32 devices in a mesh: groups: 2 (over y), terms: 4 (over z), sector: 2 (over x), rep: 2 (over core).
Axes of the slice: x: 2, y: 2, z: 4, core: 2. Of those that a mesh axis runs over, the one named last changes fastest.
Arguments:
- psi_start: float32 [4, 256, 256], P(('groups', 'sector')), parts along dimension 0, may hold values from -6 to 6
- diagonal: float32 [4, 256, 256], P(('groups', 'sector')), parts along dimension 0, may hold values from 0.5 to 3
- sector_sizes: int32 [4, 2], P('groups'), parts along dimension 0, may hold values from 64 to 256, as said below
- conn: int32 [64, 2], P(('groups', 'terms', 'rep'), 'sector'), parts along dimension 0, may hold values from 0 to 1
- left_ops: float32 [64, 2, 256, 256], P(('groups', 'terms', 'rep'), 'sector'), parts along dimension 0, may hold values from -0.375 to 0.375
- right_ops: float32 [64, 2, 256, 256], P(('groups', 'terms', 'rep'), 'sector'), parts along dimension 0, may hold values from -0.0625 to 0.0625
Outputs:
- eigvector: float32 [4, 256, 256], P(('groups', 'sector')), parts along dimension 0
- energy: float32 [2], P('groups'), parts along dimension 0
The draws below stay inside these ranges and needn't reach their ends.
There are 2 independent parts, one for each index of `groups`. The reference program is written for one: setup_inputs(seed, part) draws one part's arguments, and reference() takes and returns one part's arrays. A program takes and returns all parts, laid end to end along the dimension named above; each array names one. Nothing has to cross between parts.
Inputs may be any that keep to these rules, and one draw needn't show every extreme that they name: `sector_sizes`: both sizes of every sector lie in 64 to 256; some sector has both sizes equal to 256.
All inputs are finite; a program needn't handle non-finite values.
Results may differ from the reference program's by a relative error of at most 0.0003.
Values sent between devices are 32-bit elements; how exact they have to be, the bound alone decides.
No kernel may reach another device: no remote copies, remote signals or barrier semaphores. Data moves between devices by JAX's collectives and lax.ppermute only.
A program may use at most 64 MiB of HBM per device.

```python
import math
import jax
import jax.numpy as jnp
from jax import lax

BLK = 256
ITERS = 1
NSEC = 2
NTERM = 32


def draw_sector_sizes(key, part):
    key = jax.random.fold_in(key, 7)
    first_key, second_key = jax.random.split(key)
    values = jax.random.randint(first_key, (NSEC, 2), BLK // 4, BLK + 1, dtype=jnp.int32)
    chosen = jax.random.randint(second_key, (), 0, NSEC, dtype=jnp.int32)
    sector_ids = jnp.arange(NSEC, dtype=jnp.int32)
    return jnp.where(sector_ids[:, None] == chosen, BLK, values).astype(jnp.int32)


def touch_ends(array, stream_key, low, high):
    longest = array.shape.index(max(array.shape))
    spots = []
    for shift in (0, 1):
        where = [jax.random.randint(jax.random.fold_in(stream_key, axis), (), 0, length) for axis, length in enumerate(array.shape)]
        where[longest] = (where[longest] + shift) % array.shape[longest]
        spots.append(tuple(where))
    return array.at[spots[0]].set(low).at[spots[1]].set(high)


def level_of(own_key, shape, pieces, smallest, top_value):
    level = 1.0
    for dim, parts in pieces:
        heights = jax.random.uniform(jax.random.fold_in(jax.random.fold_in(own_key, 6), dim), (parts,), jnp.float32, smallest / len(pieces), top_value / len(pieces))
        level = level * jnp.repeat(jnp.exp(heights), shape[dim] // parts).reshape((-1,) + (1,) * (len(shape) - 1 - dim))
    return level


def scatter_about(stream_key, shape, scale, reach, pieces=(), kind=jnp.bfloat16):
    values = jax.random.normal(stream_key, shape, jnp.float32) * scale
    if len(pieces) > 0:
        values = level_of(stream_key, shape, pieces, -0.22, 0.18) * values
    return jnp.clip(values, min=-reach, max=reach).astype(kind)


def setup_inputs(seed: int = 0, part: int = 0) -> dict:
    splits = jax.random.split(jax.random.key(seed), 7)
    part_splits = jax.random.split(jax.random.fold_in(splits[6], part), 7)
    psi_start = scatter_about(part_splits[0], (NSEC, BLK, BLK), 1.0, 6.0, ((0, 2),), jnp.float32)
    diagonal = jnp.clip(0.5 + 2.5 * jax.random.uniform(part_splits[1], (NSEC, BLK, BLK), jnp.float32) ** level_of(part_splits[1], (NSEC, BLK, BLK), ((0, 2),), -0.2, 0.2), 0.5, 3.0)
    sector_sizes = draw_sector_sizes(jax.random.fold_in(jax.random.fold_in(splits[6], part), 71), part)
    conn = touch_ends(jax.random.randint(part_splits[3], (NTERM, NSEC), 0, NSEC), jax.random.fold_in(part_splits[3], 1), 0, NSEC - 1).astype(jnp.int32)
    left_ops = scatter_about(part_splits[4], (NTERM, NSEC, BLK, BLK), BLK ** -0.5, 0.375, ((0, 8), (1, 2)), jnp.float32)
    right_ops = scatter_about(part_splits[5], (NTERM, NSEC, BLK, BLK), (BLK * NTERM) ** -0.5, 0.0625, ((0, 8), (1, 2)), jnp.float32)
    return {"psi_start": psi_start, "diagonal": diagonal, "sector_sizes": sector_sizes, "conn": conn, "left_ops": left_ops, "right_ops": right_ops}


def apply_ham(vector, diagonal, live, conn, left_ops, right_ops):
    coupling = 1.0 / math.sqrt(NTERM)
    precise = lax.Precision.HIGHEST
    sector_ids = jnp.arange(NSEC, dtype=jnp.int32)

    def one_term(total, inputs):
        links, left_term, right_term = inputs
        source = vector[links]
        middle = jnp.einsum('sij,sjk->sik', left_term, source, precision=precise)
        joint = coupling * vector + jnp.einsum('sik,slk->sil', middle, right_term, precision=precise)
        returned = jnp.einsum('sji,sjk->sik', left_term, joint, precision=precise)
        returned = jnp.einsum('sik,skl->sil', returned, right_term, precision=precise)
        onehot = (links[None, :] == sector_ids[:, None]).astype(jnp.float32)
        moved = jnp.dot(onehot, returned.reshape(NSEC, BLK * BLK), precision=precise).reshape(vector.shape)
        return (total + coupling * joint + moved, None)
    total, _ = lax.scan(one_term, jnp.zeros_like(vector), (conn, left_ops, right_ops))
    return live * (diagonal * vector + total)

def reference(psi_start, diagonal, sector_sizes, conn, left_ops, right_ops):
    ncell = float(NSEC * BLK * BLK)
    row_ids = jnp.arange(BLK, dtype=jnp.int32)
    live = ((row_ids[None, :, None] < sector_sizes[:, 0][:, None, None]) & (row_ids[None, None, :] < sector_sizes[:, 1][:, None, None])).astype(jnp.float32)

    def inner(first, second):
        return jnp.sum(first * second) / ncell

    def apply(vector):
        return apply_ham(vector, diagonal, live, conn, left_ops, right_ops)
    trial = live * psi_start
    trial = trial / jnp.sqrt(inner(trial, trial))
    image = apply(trial)
    theta = inner(trial, image)
    for step in range(ITERS):
        residue = image - theta * trial
        shifted = diagonal - theta
        fresh = residue * shifted / (shifted * shifted + 1.0)
        fresh = fresh - inner(trial, fresh) * trial
        fresh = fresh / jnp.sqrt(inner(fresh, fresh))
        fresh_image = apply(fresh)
        cross = inner(trial, fresh_image)
        corner = inner(fresh, fresh_image)
        spread = (theta - corner) / 2.0
        lowest = (theta + corner) / 2.0 - jnp.sqrt(spread * spread + cross * cross)
        keep = corner - lowest
        turn = -cross
        length = jnp.sqrt(keep * keep + turn * turn)
        keep = keep / length
        turn = turn / length
        trial = keep * trial + turn * fresh
        image = keep * image + turn * fresh_image
        theta = lowest
    return (trial, jnp.reshape(theta, (1,)))
```

```python
import functools
import math

import jax
import jax.numpy as jnp
from jax import lax
from jax.experimental import pallas as pl
from jax.experimental.pallas import tpu as pltpu
from jax.sharding import PartitionSpec as P

F32 = jnp.float32
BF16 = jnp.bfloat16
PAD = 8
PARAMS = pltpu.CompilerParams(vmem_limit_bytes=40 * 1024 * 1024)
NN = (((1,), (0,)), ((), ()))
NT = (((1,), (1,)), ((), ()))
TN = (((0,), (0,)), ((), ()))


def split(x):
    high = x.astype(BF16)
    return high, (x - high.astype(F32)).astype(BF16)


def product(a, b, dims):
    dot = functools.partial(lax.dot_general, dimension_numbers=dims, preferred_element_type=F32)
    return dot(a[0], b[0]) + (dot(a[0], b[1]) + dot(a[1], b[0]))


def live_mask(sizes_ref, sector, rows, cols, first=0):
    row = lax.broadcasted_iota(jnp.int32, (rows, cols), 0) + first
    col = lax.broadcasted_iota(jnp.int32, (rows, cols), 1)
    return (row < sizes_ref[sector, 0]) & (col < sizes_ref[sector, 1])


def total(x):
    return jnp.sum(x, keepdims=True)


def image_kernel(coupling, weight, where_ref, sizes_ref, conn_ref, *refs):
    nsec = sizes_ref.shape[0]
    psi_ref, diag_ref = refs[:2]
    halves = refs[2 : 2 + 2 * (nsec - 1)]
    left_ref, right_ref, keep_ref, send_ref, full_ref, acc, high, low = refs[2 + 2 * (nsec - 1) :]
    blk = psi_ref.shape[0]
    half = blk // 2
    nterm = left_ref.shape[0]
    me, core = where_ref[0], where_ref[1]
    mine = pl.ds(pl.multiple_of(core * half, half), half)
    other = pl.ds(pl.multiple_of((1 - core) * half, half), half)
    full_ref[0] = psi_ref[...]
    for slot in range(1, nsec):
        full_ref[slot, mine, :] = halves[2 * slot - 2][...]
        full_ref[slot, other, :] = halves[2 * slot - 1][...]
    for slot in range(nsec):
        value = jnp.where(live_mask(sizes_ref, me ^ slot, blk, blk), full_ref[slot], 0.0)
        full_ref[slot] = value
        high[slot], low[slot] = split(value)
        acc[slot] = jnp.zeros((blk, blk), F32)
    own = full_ref[0]
    scalar = total(own * own * diag_ref[...]) * weight
    slots = [conn_ref[term, 0] ^ me for term in range(nterm)]
    lefts = [split(left_ref[term]) for term in range(nterm)]
    rights = [split(right_ref[term]) for term in range(nterm)]
    middles = [product(lefts[i], (high[slots[i]], low[slots[i]]), NN) for i in range(nterm)]
    joints = [coupling * own + product(split(middles[i]), rights[i], NT) for i in range(nterm)]
    for joint in joints:
        scalar = scalar + total(joint * joint)
    acc[0] = coupling * sum(joints[1:], joints[0])
    inner = [product(split(joints[i]), rights[i], NN) for i in range(nterm)]
    for i in range(nterm):
        acc[slots[i]] += product(lefts[i], split(inner[i]), TN)
    for slot in range(nsec):
        keep_ref[slot, :half, :] = acc[slot, mine, :]
        send_ref[slot, :half, :] = acc[slot, other, :]
        keep_ref[slot, half:, :] = jnp.broadcast_to(scalar, (PAD, blk))
        send_ref[slot, half:, :] = jnp.broadcast_to(scalar, (PAD, blk))


def fresh_kernel(ncell, nparts, where_ref, sizes_ref, *refs):
    parts = refs[:nparts]
    full_ref, diag_ref, fresh_ref, cross_ref = refs[nparts:]
    blk = full_ref.shape[-1]
    half = blk // 2
    me, core = where_ref[0], where_ref[1]
    first = pl.multiple_of(core * half, half)
    norm = total(full_ref[...] * full_ref[...]).reshape(1, 1) / ncell
    scale = 1.0 / jnp.sqrt(norm)
    summed = parts[0][...]
    for part in parts[1:]:
        summed = summed + part[...]
    theta = summed[half : half + 1, :1] / (ncell * norm)
    trial = full_ref[0, pl.ds(first, half), :] * scale
    diag = diag_ref[pl.ds(first, half), :]
    image = jnp.where(live_mask(sizes_ref, me, half, blk, first), diag * trial + summed[:half] * scale, 0.0)
    residue = image - theta * trial
    shifted = diag - theta
    fresh = residue * shifted / (shifted * shifted + 1.0)
    fresh_ref[...] = fresh
    row = lax.broadcasted_iota(jnp.int32, cross_ref.shape, 0)
    cross_ref[...] = jnp.where(row == 0, total(residue * fresh), theta)


def corner_kernel(coupling, weight, ncell, share, where_ref, conn_ref, *refs):
    full_ref = refs[0]
    nsec = full_ref.shape[0]
    halves = refs[1 : 1 + 2 * nsec]
    diag_ref, left_ref, right_ref, cross_ref, sums_ref, fresh_ref, info_ref, work, high, low = refs[1 + 2 * nsec :]
    blk = diag_ref.shape[0]
    half = blk // 2
    nterm = left_ref.shape[0]
    me, core = where_ref[0], where_ref[1]
    mine = pl.ds(pl.multiple_of(core * half, half), half)
    other = pl.ds(pl.multiple_of((1 - core) * half, half), half)
    for slot in range(nsec):
        work[slot, mine, :] = halves[2 * slot][...]
        work[slot, other, :] = halves[2 * slot + 1][...]
    start = full_ref[...]
    raw = work[...]
    norm = total(start * start).reshape(1, 1) / ncell
    overlap = total(start * raw).reshape(1, 1) / ncell
    fresh = raw - (overlap / norm)[None] * start
    length = total(fresh * fresh).reshape(1, 1) / ncell
    for slot in range(nsec):
        high[slot], low[slot] = split(fresh[slot])
    own = fresh[0]
    fresh_ref[...] = own
    scalar = total(own * own * diag_ref[...]) * weight
    slots = [conn_ref[term, 0] ^ me for term in range(nterm)]
    middles = [product(split(left_ref[i]), (high[slots[i]], low[slots[i]]), NN) for i in range(nterm)]
    joints = [coupling * own + product(split(middles[i]), split(right_ref[i]), NT) for i in range(nterm)]
    for joint in joints:
        scalar = scalar + total(joint * joint)
    row = lax.broadcasted_iota(jnp.int32, sums_ref.shape, 0)
    cross = cross_ref[...][:1, :1] * share
    sums_ref[...] = jnp.where(row == 0, scalar, cross)
    info_ref[...] = jnp.where(row == 0, norm, jnp.where(row == 1, length, cross_ref[...][1:2, :1]))


def result_kernel(ncell, sums_ref, info_ref, full_ref, fresh_ref, vector_ref, energy_ref):
    sums, info = sums_ref[...], info_ref[...]
    norm, length, theta = info[0:1, :1], info[1:2, :1], info[2:3, :1]
    corner = sums[0:1, :1] / (ncell * length)
    cross = sums[1:2, :1] / (ncell * jnp.sqrt(length))
    spread = (theta - corner) / 2.0
    lowest = (theta + corner) / 2.0 - jnp.sqrt(spread * spread + cross * cross)
    keep = corner - lowest
    turn = -cross
    size = jnp.sqrt(keep * keep + turn * turn)
    keep = keep / size
    turn = turn / size
    vector_ref[0] = (keep / jnp.sqrt(norm)) * full_ref[0] + (turn / jnp.sqrt(length)) * fresh_ref[...]
    energy_ref[...] = jnp.broadcast_to(lowest, energy_ref.shape)


def across(x, axis, step):
    size = lax.axis_size(axis)
    return lax.ppermute(x, axis, [(i, i ^ step) for i in range(size)])


def body(psi_start, diagonal, sector_sizes, conn, left_ops, right_ops):
    blk = psi_start.shape[-1]
    half = blk // 2
    nterm_dev = conn.shape[0]
    nsec, nz, nrep = lax.axis_size("sector"), lax.axis_size("terms"), lax.axis_size("rep")
    coupling = 1.0 / math.sqrt(nterm_dev * nz * nrep)
    ncell = float(nsec * blk * blk)
    me, core = lax.axis_index("sector"), lax.axis_index("rep")
    where = jnp.stack([me, core]).astype(jnp.int32)
    psi, diag = psi_start[0], diagonal[0]
    left, right = left_ops[:, 0], right_ops[:, 0]
    vmem, smem = pl.BlockSpec(memory_space=pltpu.VMEM), pl.BlockSpec(memory_space=pltpu.SMEM)

    mine = lax.dynamic_slice_in_dim(psi, core * half, half, 0)
    halves = []
    for step in range(1, nsec):
        near = across(mine, "sector", step)
        halves += [near, across(near, "rep", 1)]
    keep, send, full = pl.pallas_call(
        functools.partial(image_kernel, coupling, 1.0 / (nz * nrep)),
        out_shape=[
            jax.ShapeDtypeStruct((nsec, half + PAD, blk), F32),
            jax.ShapeDtypeStruct((nsec, half + PAD, blk), F32),
            jax.ShapeDtypeStruct((nsec, blk, blk), F32),
        ],
        in_specs=[smem] * 3 + [vmem] * (len(halves) + 4),
        out_specs=[vmem] * 3,
        scratch_shapes=[
            pltpu.VMEM((nsec, blk, blk), F32),
            pltpu.VMEM((nsec, blk, blk), BF16),
            pltpu.VMEM((nsec, blk, blk), BF16),
        ],
        compiler_params=PARAMS,
        name="image",
    )(where, sector_sizes, conn, psi, diag, *halves, left, right)

    chip = keep + across(send, "rep", 1)
    part = chip[0]
    for step in range(1, nsec):
        part = part + across(chip[step], "sector", step)
    parts = [part] + [across(part, "terms", step) for step in range(1, nz)]
    fresh, cross = pl.pallas_call(
        functools.partial(fresh_kernel, ncell, nz),
        out_shape=[jax.ShapeDtypeStruct((half, blk), F32), jax.ShapeDtypeStruct((8, 128), F32)],
        in_specs=[smem] * 2 + [vmem] * (nz + 2),
        out_specs=[vmem] * 2,
        compiler_params=PARAMS,
        name="fresh",
    )(where, sector_sizes, *parts, full, diag)

    halves = []
    for step in range(nsec):
        near = across(fresh, "sector", step) if step else fresh
        halves += [near, across(near, "rep", 1)]
    sums, direction, info = pl.pallas_call(
        functools.partial(corner_kernel, coupling, 1.0 / (nz * nrep), ncell, 1.0 / nz),
        out_shape=[
            jax.ShapeDtypeStruct((8, 128), F32),
            jax.ShapeDtypeStruct((blk, blk), F32),
            jax.ShapeDtypeStruct((8, 128), F32),
        ],
        in_specs=[smem] * 2 + [vmem] * (len(halves) + 5),
        out_specs=[vmem] * 3,
        scratch_shapes=[
            pltpu.VMEM((nsec, blk, blk), F32),
            pltpu.VMEM((nsec, blk, blk), BF16),
            pltpu.VMEM((nsec, blk, blk), BF16),
        ],
        compiler_params=PARAMS,
        name="corner",
    )(where, conn, full, *halves, diag, left, right, cross)

    for axis in ("rep", "sector", "terms"):
        step = 1
        while step < lax.axis_size(axis):
            sums = sums + across(sums, axis, step)
            step *= 2
    vector, energy = pl.pallas_call(
        functools.partial(result_kernel, ncell),
        out_shape=[jax.ShapeDtypeStruct((1, blk, blk), F32), jax.ShapeDtypeStruct((8, 128), F32)],
        in_specs=[vmem] * 4,
        out_specs=[vmem] * 2,
        compiler_params=PARAMS,
        name="result",
    )(sums, info, full, direction)
    return vector, energy[0, :1]


def solution(mesh):
    in_specs = (
        P(("groups", "sector"), None, None),
        P(("groups", "sector"), None, None),
        P("groups", None),
        P(("groups", "terms", "rep"), "sector"),
        P(("groups", "terms", "rep"), "sector", None, None),
        P(("groups", "terms", "rep"), "sector", None, None),
    )
    out_specs = (P(("groups", "sector"), None, None), P("groups"))
    return jax.shard_map(body, mesh=mesh, in_specs=in_specs, out_specs=out_specs, check_vma=False)
```

```python
import functools
import math

import jax
import jax.numpy as jnp
from jax import lax
from jax.experimental import pallas as pl
from jax.experimental.pallas import tpu as pltpu
from jax.sharding import PartitionSpec as P

F32 = jnp.float32
BF16 = jnp.bfloat16
PREPARE = 49
LANES = 128
PAD = 8
PARAMS = pltpu.CompilerParams(vmem_limit_bytes=40 * 1024 * 1024)
NN = (((1,), (0,)), ((), ()))
NT = (((1,), (1,)), ((), ()))


def split(x):
    high = x.astype(BF16)
    return high, (x - high.astype(F32)).astype(BF16)


def product(a, b, dims):
    dot = functools.partial(lax.dot_general, dimension_numbers=dims, preferred_element_type=F32)
    return dot(a[0], b[0]) + (dot(a[0], b[1]) + dot(a[1], b[0]))


def live_mask(sizes_ref, sector, first, rows, cols):
    row = lax.broadcasted_iota(jnp.int32, (rows, cols), 0) + first
    col = lax.broadcasted_iota(jnp.int32, (rows, cols), 1)
    return ((row < sizes_ref[sector, 0]) & (col < sizes_ref[sector, 1])).astype(F32)


def total(x):
    return jnp.sum(x, keepdims=True)


def halves_of(half):
    core = lax.axis_index("rep")
    mine = pl.ds(pl.multiple_of(core * half, half), half)
    other = pl.ds(pl.multiple_of((1 - core) * half, half), half)
    return mine, other


def prepare_kernel(weight, sizes_ref, conn_ref, psi_hbm, diag_hbm, left_hbm, right_hbm, *refs):
    lh, ll, th, tl, rh, rl, mask_ref, own_ref, slot_ref, stat_ref, psi, diag, left, right, vector_sem, left_sem, right_sem = refs
    nterm = left.shape[0]
    vectors = [
        pltpu.make_async_copy(psi_hbm.at[0], psi, vector_sem.at[0]),
        pltpu.make_async_copy(diag_hbm.at[0], diag, vector_sem.at[1]),
    ]
    lefts = [pltpu.make_async_copy(left_hbm.at[i, 0], left.at[i], left_sem.at[i]) for i in range(nterm)]
    rights = [pltpu.make_async_copy(right_hbm.at[i, 0], right.at[i], right_sem.at[i]) for i in range(nterm)]
    for copy in vectors + lefts + rights:
        copy.start()
    me = lax.axis_index("sector")
    nsec, half, blk = mask_ref.shape
    first = lax.axis_index("rep") * half
    for slot in range(nsec):
        mask_ref[slot] = live_mask(sizes_ref, me ^ slot, first, half, blk)
    for term in range(nterm):
        slot_ref[term] = jnp.full(slot_ref.shape[1:], conn_ref[term] ^ me, jnp.int32)
    for copy in vectors:
        copy.wait()
    own = psi[...] * live_mask(sizes_ref, me, 0, blk, blk)
    own_ref[...] = own
    square = own * own
    row = lax.broadcasted_iota(jnp.int32, stat_ref.shape, 0)
    stat_ref[...] = jnp.where(row == 0, total(square), total(square * diag[...]) * weight)
    for term in range(nterm):
        lefts[term].wait()
        value = left[term]
        lh[term], ll[term] = split(value)
        th[term], tl[term] = split(value.T)
    for term in range(nterm):
        rights[term].wait()
        rh[term], rl[term] = split(right[term])


def pick(slot_ref, term, blocks):
    blk = blocks[0].shape[0]
    slot = jnp.broadcast_to(slot_ref[term, :1, :], (blk, blk))
    value = blocks[0]
    for index in range(1, len(blocks)):
        value = jnp.where(slot == index, blocks[index], value)
    return value


def image_kernel(coupling, ncell, nsec, *refs):
    halves = refs[: 2 * (nsec - 1)]
    own_ref, slot_ref, stat_ref = refs[2 * (nsec - 1) : 2 * (nsec - 1) + 3]
    lh, ll, th, tl, rh, rl, keep_ref, send_ref, full_ref, norm_ref, acc = refs[2 * (nsec - 1) + 3 :]
    blk = own_ref.shape[0]
    half = blk // 2
    nterm = lh.shape[0]
    mine, other = halves_of(half)
    own = own_ref[...]
    full_ref[0] = own
    for slot in range(1, nsec):
        full_ref[slot, mine, :] = halves[2 * slot - 2][...]
        full_ref[slot, other, :] = halves[2 * slot - 1][...]
    blocks = [own] + [full_ref[slot] for slot in range(1, nsec)]
    norm = stat_ref[:1, :1]
    for block in blocks[1:]:
        norm = norm + total(block * block)
    norm_ref[...] = jnp.broadcast_to(norm / ncell, norm_ref.shape)
    terms = range(nterm)
    middles = [product((lh[i], ll[i]), split(pick(slot_ref, i, blocks)), NN) for i in terms]
    joints = [coupling * own + product(split(middles[i]), (rh[i], rl[i]), NT) for i in terms]
    squares = joints[0] * joints[0]
    for joint in joints[1:]:
        squares = squares + joint * joint
    scalar = stat_ref[1:2, :1] + total(squares)
    inner = [product(split(joints[i]), (rh[i], rl[i]), NN) for i in terms]
    returned = [product((th[i], tl[i]), split(inner[i]), NN) for i in terms]
    for slot in range(nsec):
        value = coupling * sum(joints[1:], joints[0]) if slot == 0 else jnp.zeros((blk, blk), F32)
        for i in terms:
            target = jnp.broadcast_to(slot_ref[i, :1, :], (blk, blk))
            value = value + jnp.where(target == slot, returned[i], 0.0)
        acc[slot] = value
        for ref, rows in ((keep_ref, mine), (send_ref, other)):
            for tile in range(blk // LANES):
                ref[slot, tile * half : (tile + 1) * half, :] = acc[slot, rows, tile * LANES : (tile + 1) * LANES]
            ref[slot, blk // LANES * half :, :] = jnp.broadcast_to(scalar, (PAD, LANES))


def fresh_kernel(ncell, nparts, *refs):
    parts = refs[:nparts]
    full_ref, mask_ref, diag_ref, norm_ref, fresh_ref, cross_ref = refs[nparts:]
    half, blk = fresh_ref.shape
    mine, _ = halves_of(half)
    norm = norm_ref[:1, :1]
    scale = 1.0 / jnp.sqrt(norm)
    summed = parts[0][...]
    for part in parts[1:]:
        summed = summed + part[...]
    tiles = blk // LANES
    theta = summed[tiles * half : tiles * half + 1, :1] / (ncell * norm)
    summed = jnp.concatenate([summed[tile * half : (tile + 1) * half] for tile in range(tiles)], axis=1)
    trial = full_ref[0, mine, :] * scale
    diag = diag_ref[mine, :]
    image = (diag * trial + summed * scale) * mask_ref[0]
    residue = image - theta * trial
    shifted = diag - theta
    fresh = residue * shifted / (shifted * shifted + 1.0)
    fresh_ref[...] = fresh
    row = lax.broadcasted_iota(jnp.int32, cross_ref.shape, 0)
    cross_ref[...] = jnp.where(row == 0, total(residue * fresh), theta)


def corner_kernel(coupling, weight, ncell, share, nsec, *refs):
    halves = refs[: 2 * nsec]
    full_ref, diag_ref, norm_ref, cross_ref, slot_ref, lh, ll, rh, rl = refs[2 * nsec : 2 * nsec + 9]
    sums_ref, fresh_ref, info_ref, work = refs[2 * nsec + 9 :]
    blk = diag_ref.shape[0]
    nterm = lh.shape[0]
    mine, other = halves_of(blk // 2)
    for slot in range(nsec):
        work[slot, mine, :] = halves[2 * slot][...]
        work[slot, other, :] = halves[2 * slot + 1][...]
    norm = norm_ref[:1, :1]
    start = [full_ref[slot] for slot in range(nsec)]
    raw = [work[slot] for slot in range(nsec)]
    overlap = start[0] * raw[0]
    for slot in range(1, nsec):
        overlap = overlap + start[slot] * raw[slot]
    overlap = total(overlap) / (ncell * norm)
    fresh = [raw[slot] - overlap * start[slot] for slot in range(nsec)]
    length = fresh[0] * fresh[0]
    for slot in range(1, nsec):
        length = length + fresh[slot] * fresh[slot]
    length = total(length) / ncell
    own = fresh[0]
    fresh_ref[...] = own
    terms = range(nterm)
    middles = [product((lh[i], ll[i]), split(pick(slot_ref, i, fresh)), NN) for i in terms]
    joints = [coupling * own + product(split(middles[i]), (rh[i], rl[i]), NT) for i in terms]
    squares = weight * own * own * diag_ref[...]
    for joint in joints:
        squares = squares + joint * joint
    row = lax.broadcasted_iota(jnp.int32, sums_ref.shape, 0)
    sums_ref[...] = jnp.where(row == 0, total(squares), cross_ref[:1, :1] * share)
    info_ref[...] = jnp.where(row == 0, norm, jnp.where(row == 1, length, cross_ref[1:2, :1]))


def result_kernel(ncell, sums_ref, info_ref, full_ref, fresh_ref, vector_ref, energy_ref):
    sums, info = sums_ref[...], info_ref[...]
    norm, length, theta = info[0:1, :1], info[1:2, :1], info[2:3, :1]
    corner = sums[0:1, :1] / (ncell * length)
    cross = sums[1:2, :1] / (ncell * jnp.sqrt(length))
    spread = (theta - corner) / 2.0
    lowest = (theta + corner) / 2.0 - jnp.sqrt(spread * spread + cross * cross)
    keep = corner - lowest
    turn = -cross
    size = jnp.sqrt(keep * keep + turn * turn)
    keep = keep / size
    turn = turn / size
    vector_ref[0] = (keep / jnp.sqrt(norm)) * full_ref[0] + (turn / jnp.sqrt(length)) * fresh_ref[...]
    energy_ref[0] = jnp.sum(lowest)


def across(x, axis, step):
    size = lax.axis_size(axis)
    return lax.ppermute(x, axis, [(i, i ^ step) for i in range(size)])


def diagonally(x, axis, step):
    size = lax.axis_size(axis)
    return lax.ppermute(x, (axis, "rep"), [(2 * i + c, 2 * (i ^ step) + 1 - c) for i in range(size) for c in range(2)])


def body(psi_start, diagonal, sector_sizes, conn, left_ops, right_ops):
    blk = psi_start.shape[-1]
    half = blk // 2
    nterm_dev = conn.shape[0]
    nsec, nz, nrep = lax.axis_size("sector"), lax.axis_size("terms"), lax.axis_size("rep")
    coupling = 1.0 / math.sqrt(nterm_dev * nz * nrep)
    weight = 1.0 / (nz * nrep)
    ncell = float(nsec * blk * blk)
    core = lax.axis_index("rep")
    psi, diag = psi_start[0], diagonal[0]
    vmem, smem, hbm = (pl.BlockSpec(memory_space=space) for space in (pltpu.VMEM, pltpu.SMEM, pltpu.HBM))
    shape = jax.ShapeDtypeStruct

    mine = lax.dynamic_slice_in_dim(psi, core * half, half, 0)
    halves = []
    for step in range(1, nsec):
        near = across(mine, "sector", step)
        halves.append(near)

    operator = (nterm_dev, blk, blk)
    *ops, mask, own, slots, stat = pl.pallas_call(
        functools.partial(prepare_kernel, weight),
        out_shape=[shape(operator, BF16)] * 6
        + [shape((nsec, half, blk), F32), shape((blk, blk), F32), shape((nterm_dev, 8, blk), jnp.int32), shape((8, 128), F32)],
        in_specs=[smem] * 2 + [hbm] * 4,
        out_specs=[vmem] * 10,
        scratch_shapes=[
            pltpu.VMEM((blk, blk), F32),
            pltpu.VMEM((blk, blk), F32),
            pltpu.VMEM(operator, F32),
            pltpu.VMEM(operator, F32),
            pltpu.SemaphoreType.DMA((2,)),
            pltpu.SemaphoreType.DMA((nterm_dev,)),
            pltpu.SemaphoreType.DMA((nterm_dev,)),
        ],
        compiler_params=pltpu.CompilerParams(vmem_limit_bytes=PREPARE * 1024 * 1024),
        name="prepare",
    )(sector_sizes, conn[:, 0], psi_start, diagonal, left_ops, right_ops)
    lh, ll, th, tl, rh, rl = ops
    masked = [near * mask[slot] for slot, near in enumerate(halves, 1)]
    halves = [part for near in masked for part in (near, across(near, "rep", 1))]

    keep, send, full, norm = pl.pallas_call(
        functools.partial(image_kernel, coupling, ncell, nsec),
        out_shape=[
            shape((nsec, blk // LANES * half + PAD, LANES), F32),
            shape((nsec, blk // LANES * half + PAD, LANES), F32),
            shape((nsec, blk, blk), F32),
            shape((8, 128), F32),
        ],
        in_specs=[vmem] * (len(halves) + 9),
        out_specs=[vmem] * 4,
        scratch_shapes=[pltpu.VMEM((nsec, blk, blk), F32)],
        compiler_params=PARAMS,
        name="image",
    )(*halves, own, slots, stat, lh, ll, th, tl, rh, rl)

    chip = keep + across(send, "rep", 1)
    part = chip[0]
    for step in range(1, nsec):
        part = part + across(chip[step], "sector", step)
    parts = [part] + [across(part, "terms", step) for step in range(1, nz)]
    fresh, cross = pl.pallas_call(
        functools.partial(fresh_kernel, ncell, nz),
        out_shape=[shape((half, blk), F32), shape((8, 128), F32)],
        in_specs=[vmem] * (nz + 4),
        out_specs=[vmem] * 2,
        compiler_params=PARAMS,
        name="fresh",
    )(*parts, full, mask, diag, norm)

    halves = []
    for step in range(nsec):
        near = across(fresh, "sector", step) if step else fresh
        halves += [near, across(near, "rep", 1)]
    sums, direction, info = pl.pallas_call(
        functools.partial(corner_kernel, coupling, weight, ncell, 1.0 / nz, nsec),
        out_shape=[shape((8, 128), F32), shape((blk, blk), F32), shape((8, 128), F32)],
        in_specs=[vmem] * (len(halves) + 9),
        out_specs=[vmem] * 3,
        scratch_shapes=[pltpu.VMEM((nsec, blk, blk), F32)],
        compiler_params=PARAMS,
        name="corner",
    )(*halves, full, diag, norm, cross, slots, lh, ll, rh, rl)

    sums = sums + across(sums, "rep", 1)
    for axis in ("sector", "terms"):
        parts = [diagonally(sums, axis, step) for step in range(1, lax.axis_size(axis))]
        sums = functools.reduce(lambda x, y: x + y, parts, sums)
    vector, energy = pl.pallas_call(
        functools.partial(result_kernel, ncell),
        out_shape=[shape((1, blk, blk), F32), shape((1,), F32)],
        in_specs=[vmem] * 4,
        out_specs=[vmem, smem],
        compiler_params=PARAMS,
        name="result",
    )(sums, info, full, direction)
    return vector, energy


def solution(mesh):
    in_specs = (
        P(("groups", "sector"), None, None),
        P(("groups", "sector"), None, None),
        P("groups", None),
        P(("groups", "terms", "rep"), "sector"),
        P(("groups", "terms", "rep"), "sector", None, None),
        P(("groups", "terms", "rep"), "sector", None, None),
    )
    out_specs = (P(("groups", "sector"), None, None), P("groups"))
    return jax.shard_map(body, mesh=mesh, in_specs=in_specs, out_specs=out_specs, check_vma=False)
```

```python
import functools
import math

import jax
import jax.numpy as jnp
from jax import lax
from jax.experimental import pallas as pl
from jax.experimental.pallas import tpu as pltpu
from jax.sharding import PartitionSpec as P

F32 = jnp.float32
BF16 = jnp.bfloat16
PREPARE = 49
LANES = 128
PAD = 8
PARAMS = pltpu.CompilerParams(vmem_limit_bytes=40 * 1024 * 1024)
NN = (((1,), (0,)), ((), ()))
NT = (((1,), (1,)), ((), ()))


def split(x):
    high = x.astype(BF16)
    return high, (x - high.astype(F32)).astype(BF16)


def product(a, b, dims):
    dot = functools.partial(lax.dot_general, dimension_numbers=dims, preferred_element_type=F32)
    return dot(a[0], b[0]) + (dot(a[0], b[1]) + dot(a[1], b[0]))


def live_mask(sizes_ref, sector, first, rows, cols):
    row = lax.broadcasted_iota(jnp.int32, (rows, cols), 0) + first
    col = lax.broadcasted_iota(jnp.int32, (rows, cols), 1)
    return ((row < sizes_ref[sector, 0]) & (col < sizes_ref[sector, 1])).astype(F32)


def total(x):
    return jnp.sum(x, keepdims=True)


def halves_of(half):
    core = lax.axis_index("rep")
    mine = pl.ds(pl.multiple_of(core * half, half), half)
    other = pl.ds(pl.multiple_of((1 - core) * half, half), half)
    return mine, other


def prepare_kernel(weight, sizes_ref, conn_ref, psi_hbm, diag_hbm, left_hbm, right_hbm, *refs):
    lh, ll, th, tl, rh, rl, mask_ref, own_ref, slot_ref, stat_ref, psi, diag, left, right, vector_sem, left_sem, right_sem = refs
    nterm = left.shape[0]
    vectors = [
        pltpu.make_async_copy(psi_hbm.at[0], psi, vector_sem.at[0]),
        pltpu.make_async_copy(diag_hbm.at[0], diag, vector_sem.at[1]),
    ]
    lefts = [pltpu.make_async_copy(left_hbm.at[i, 0], left.at[i], left_sem.at[i]) for i in range(nterm)]
    rights = [pltpu.make_async_copy(right_hbm.at[i, 0], right.at[i], right_sem.at[i]) for i in range(nterm)]
    for copy in vectors + lefts + rights:
        copy.start()
    me = lax.axis_index("sector")
    nsec, half, blk = mask_ref.shape
    first = lax.axis_index("rep") * half
    for slot in range(nsec):
        mask_ref[slot] = live_mask(sizes_ref, me ^ slot, first, half, blk)
    for term in range(nterm):
        slot_ref[term] = jnp.full(slot_ref.shape[1:], conn_ref[term] ^ me, jnp.int32)
    for copy in vectors:
        copy.wait()
    own = psi[...] * live_mask(sizes_ref, me, 0, blk, blk)
    own_ref[...] = own
    square = own * own
    row = lax.broadcasted_iota(jnp.int32, stat_ref.shape, 0)
    stat_ref[...] = jnp.where(row == 0, total(square), total(square * diag[...]) * weight)
    for term in range(nterm):
        lefts[term].wait()
        value = left[term]
        lh[term], ll[term] = split(value)
        th[term], tl[term] = split(value.T)
    for term in range(nterm):
        rights[term].wait()
        rh[term], rl[term] = split(right[term])


def pick(slot_ref, term, blocks):
    blk = blocks[0].shape[0]
    slot = jnp.broadcast_to(slot_ref[term, :1, :], (blk, blk))
    value = blocks[0]
    for index in range(1, len(blocks)):
        value = jnp.where(slot == index, blocks[index], value)
    return value


def image_kernel(coupling, ncell, nsec, *refs):
    halves = refs[: 2 * (nsec - 1)]
    own_ref, slot_ref, stat_ref = refs[2 * (nsec - 1) : 2 * (nsec - 1) + 3]
    lh, ll, th, tl, rh, rl, keep_ref, send_ref, full_ref, norm_ref, acc = refs[2 * (nsec - 1) + 3 :]
    blk = own_ref.shape[0]
    half = blk // 2
    nterm = lh.shape[0]
    mine, other = halves_of(half)
    own = own_ref[...]
    full_ref[0] = own
    for slot in range(1, nsec):
        full_ref[slot, mine, :] = halves[2 * slot - 2][...]
        full_ref[slot, other, :] = halves[2 * slot - 1][...]
    blocks = [own] + [full_ref[slot] for slot in range(1, nsec)]
    norm = stat_ref[:1, :1]
    for block in blocks[1:]:
        norm = norm + total(block * block)
    norm_ref[...] = jnp.broadcast_to(norm / ncell, norm_ref.shape)
    terms = range(nterm)
    middles = [product((lh[i], ll[i]), split(pick(slot_ref, i, blocks)), NN) for i in terms]
    joints = [coupling * own + product(split(middles[i]), (rh[i], rl[i]), NT) for i in terms]
    squares = joints[0] * joints[0]
    for joint in joints[1:]:
        squares = squares + joint * joint
    scalar = stat_ref[1:2, :1] + total(squares)
    inner = [product(split(joints[i]), (rh[i], rl[i]), NN) for i in terms]
    returned = [product((th[i], tl[i]), split(inner[i]), NN) for i in terms]
    for slot in range(nsec):
        value = coupling * sum(joints[1:], joints[0]) if slot == 0 else jnp.zeros((blk, blk), F32)
        for i in terms:
            target = jnp.broadcast_to(slot_ref[i, :1, :], (blk, blk))
            value = value + jnp.where(target == slot, returned[i], 0.0)
        acc[slot] = value
        for ref, rows in ((keep_ref, mine), (send_ref, other)):
            for tile in range(blk // LANES):
                ref[slot, tile * half : (tile + 1) * half, :] = acc[slot, rows, tile * LANES : (tile + 1) * LANES]
            ref[slot, blk // LANES * half :, :] = jnp.broadcast_to(scalar, (PAD, LANES))


def fresh_kernel(ncell, ntile, *refs):
    parts = refs[: 2 * ntile]
    full_ref, mask_ref, diag_ref, norm_ref, fresh_ref, cross_ref = refs[2 * ntile :]
    half = fresh_ref.shape[0]
    mine, _ = halves_of(half)
    norm = norm_ref[:1, :1]
    scale = 1.0 / jnp.sqrt(norm)
    sums = [parts[2 * tile][...] + parts[2 * tile + 1][...] for tile in range(ntile)]
    theta = sums[-1][half : half + 1, :1] / (ncell * norm)
    summed = jnp.concatenate([tile[:half] for tile in sums], axis=1)
    trial = full_ref[0, mine, :] * scale
    diag = diag_ref[mine, :]
    image = (diag * trial + summed * scale) * mask_ref[0]
    residue = image - theta * trial
    shifted = diag - theta
    fresh = residue * shifted / (shifted * shifted + 1.0)
    fresh_ref[...] = fresh
    row = lax.broadcasted_iota(jnp.int32, cross_ref.shape, 0)
    cross_ref[...] = jnp.where(row == 0, total(residue * fresh), theta)


def corner_kernel(coupling, weight, ncell, share, nsec, *refs):
    halves = refs[: 2 * nsec]
    full_ref, diag_ref, norm_ref, cross_ref, slot_ref, lh, ll, rh, rl = refs[2 * nsec : 2 * nsec + 9]
    sums_ref, fresh_ref, info_ref, work = refs[2 * nsec + 9 :]
    blk = diag_ref.shape[0]
    nterm = lh.shape[0]
    mine, other = halves_of(blk // 2)
    for slot in range(nsec):
        work[slot, mine, :] = halves[2 * slot][...]
        work[slot, other, :] = halves[2 * slot + 1][...]
    norm = norm_ref[:1, :1]
    start = [full_ref[slot] for slot in range(nsec)]
    raw = [work[slot] for slot in range(nsec)]
    overlap = start[0] * raw[0]
    for slot in range(1, nsec):
        overlap = overlap + start[slot] * raw[slot]
    overlap = total(overlap) / (ncell * norm)
    fresh = [raw[slot] - overlap * start[slot] for slot in range(nsec)]
    length = fresh[0] * fresh[0]
    for slot in range(1, nsec):
        length = length + fresh[slot] * fresh[slot]
    length = total(length) / ncell
    own = fresh[0]
    fresh_ref[...] = own
    terms = range(nterm)
    middles = [product((lh[i], ll[i]), split(pick(slot_ref, i, fresh)), NN) for i in terms]
    joints = [coupling * own + product(split(middles[i]), (rh[i], rl[i]), NT) for i in terms]
    squares = weight * own * own * diag_ref[...]
    for joint in joints:
        squares = squares + joint * joint
    row = lax.broadcasted_iota(jnp.int32, sums_ref.shape, 0)
    sums_ref[...] = jnp.where(row == 0, total(squares), cross_ref[:1, :1] * share)
    info_ref[...] = jnp.where(row == 0, norm, jnp.where(row == 1, length, cross_ref[1:2, :1]))


def result_kernel(ncell, sums_ref, info_ref, full_ref, fresh_ref, vector_ref, energy_ref):
    sums, info = sums_ref[...], info_ref[...]
    norm, length, theta = info[0:1, :1], info[1:2, :1], info[2:3, :1]
    corner = sums[0:1, :1] / (ncell * length)
    cross = sums[1:2, :1] / (ncell * jnp.sqrt(length))
    spread = (theta - corner) / 2.0
    lowest = (theta + corner) / 2.0 - jnp.sqrt(spread * spread + cross * cross)
    keep = corner - lowest
    turn = -cross
    size = jnp.sqrt(keep * keep + turn * turn)
    keep = keep / size
    turn = turn / size
    vector_ref[0] = (keep / jnp.sqrt(norm)) * full_ref[0] + (turn / jnp.sqrt(length)) * fresh_ref[...]
    energy_ref[0] = jnp.sum(lowest)


def across(x, axis, step):
    size = lax.axis_size(axis)
    return lax.ppermute(x, axis, [(i, i ^ step) for i in range(size)])


def diagonally(x, axis, step):
    size = lax.axis_size(axis)
    return lax.ppermute(x, (axis, "rep"), [(2 * i + c, 2 * (i ^ step) + 1 - c) for i in range(size) for c in range(2)])


def body(psi_start, diagonal, sector_sizes, conn, left_ops, right_ops):
    blk = psi_start.shape[-1]
    half = blk // 2
    nterm_dev = conn.shape[0]
    nsec, nz, nrep = lax.axis_size("sector"), lax.axis_size("terms"), lax.axis_size("rep")
    coupling = 1.0 / math.sqrt(nterm_dev * nz * nrep)
    weight = 1.0 / (nz * nrep)
    ncell = float(nsec * blk * blk)
    core = lax.axis_index("rep")
    psi, diag = psi_start[0], diagonal[0]
    vmem, smem, hbm = (pl.BlockSpec(memory_space=space) for space in (pltpu.VMEM, pltpu.SMEM, pltpu.HBM))
    shape = jax.ShapeDtypeStruct

    mine = lax.dynamic_slice_in_dim(psi, core * half, half, 0)
    halves = []
    for step in range(1, nsec):
        near = across(mine, "sector", step)
        halves.append(near)

    operator = (nterm_dev, blk, blk)
    *ops, mask, own, slots, stat = pl.pallas_call(
        functools.partial(prepare_kernel, weight),
        out_shape=[shape(operator, BF16)] * 6
        + [shape((nsec, half, blk), F32), shape((blk, blk), F32), shape((nterm_dev, 8, blk), jnp.int32), shape((8, 128), F32)],
        in_specs=[smem] * 2 + [hbm] * 4,
        out_specs=[vmem] * 10,
        scratch_shapes=[
            pltpu.VMEM((blk, blk), F32),
            pltpu.VMEM((blk, blk), F32),
            pltpu.VMEM(operator, F32),
            pltpu.VMEM(operator, F32),
            pltpu.SemaphoreType.DMA((2,)),
            pltpu.SemaphoreType.DMA((nterm_dev,)),
            pltpu.SemaphoreType.DMA((nterm_dev,)),
        ],
        compiler_params=pltpu.CompilerParams(vmem_limit_bytes=PREPARE * 1024 * 1024),
        name="prepare",
    )(sector_sizes, conn[:, 0], psi_start, diagonal, left_ops, right_ops)
    lh, ll, th, tl, rh, rl = ops
    masked = [near * mask[slot] for slot, near in enumerate(halves, 1)]
    halves = [part for near in masked for part in (near, across(near, "rep", 1))]

    keep, send, full, norm = pl.pallas_call(
        functools.partial(image_kernel, coupling, ncell, nsec),
        out_shape=[
            shape((nsec, blk // LANES * half + PAD, LANES), F32),
            shape((nsec, blk // LANES * half + PAD, LANES), F32),
            shape((nsec, blk, blk), F32),
            shape((8, 128), F32),
        ],
        in_specs=[vmem] * (len(halves) + 9),
        out_specs=[vmem] * 4,
        scratch_shapes=[pltpu.VMEM((nsec, blk, blk), F32)],
        compiler_params=PARAMS,
        name="image",
    )(*halves, own, slots, stat, lh, ll, th, tl, rh, rl)

    chip = keep + across(send, "rep", 1)
    ntile = blk // LANES
    bounds = [tile * half for tile in range(ntile)] + [ntile * half + PAD]
    parts = []
    for tile, (low, high) in enumerate(zip(bounds[:-1], bounds[1:])):
        part = chip[0, low:high]
        for step in range(1, nsec):
            part = part + across(chip[step, low:high], "sector", step)
        steps = [1 << bit for bit in range(nz.bit_length() - 1)]
        if tile % 2:
            steps.reverse()
        for step in steps[:-1]:
            part = part + across(part, "terms", step)
        parts += [part, across(part, "terms", steps[-1])]
    fresh, cross = pl.pallas_call(
        functools.partial(fresh_kernel, ncell, ntile),
        out_shape=[shape((half, blk), F32), shape((8, 128), F32)],
        in_specs=[vmem] * (len(parts) + 4),
        out_specs=[vmem] * 2,
        compiler_params=PARAMS,
        name="fresh",
    )(*parts, full, mask, diag, norm)

    halves = []
    for step in range(nsec):
        near = across(fresh, "sector", step) if step else fresh
        halves += [near, across(near, "rep", 1)]
    sums, direction, info = pl.pallas_call(
        functools.partial(corner_kernel, coupling, weight, ncell, 1.0 / nz, nsec),
        out_shape=[shape((8, 128), F32), shape((blk, blk), F32), shape((8, 128), F32)],
        in_specs=[vmem] * (len(halves) + 9),
        out_specs=[vmem] * 3,
        scratch_shapes=[pltpu.VMEM((nsec, blk, blk), F32)],
        compiler_params=PARAMS,
        name="corner",
    )(*halves, full, diag, norm, cross, slots, lh, ll, rh, rl)

    sums = sums + across(sums, "rep", 1)
    for axis in ("sector", "terms"):
        parts = [diagonally(sums, axis, step) for step in range(1, lax.axis_size(axis))]
        sums = functools.reduce(lambda x, y: x + y, parts, sums)
    vector, energy = pl.pallas_call(
        functools.partial(result_kernel, ncell),
        out_shape=[shape((1, blk, blk), F32), shape((1,), F32)],
        in_specs=[vmem] * 4,
        out_specs=[vmem, smem],
        compiler_params=PARAMS,
        name="result",
    )(sums, info, full, direction)
    return vector, energy


def solution(mesh):
    in_specs = (
        P(("groups", "sector"), None, None),
        P(("groups", "sector"), None, None),
        P("groups", None),
        P(("groups", "terms", "rep"), "sector"),
        P(("groups", "terms", "rep"), "sector", None, None),
        P(("groups", "terms", "rep"), "sector", None, None),
    )
    out_specs = (P(("groups", "sector"), None, None), P("groups"))
    return jax.shard_map(body, mesh=mesh, in_specs=in_specs, out_specs=out_specs, check_vma=False)
```

```python
import functools
import math

import jax
import jax.numpy as jnp
from jax import lax
from jax.experimental import pallas as pl
from jax.experimental.pallas import tpu as pltpu
from jax.sharding import PartitionSpec as P

F32 = jnp.float32
BF16 = jnp.bfloat16
PREPARE = 49
LANES = 128
PAD = 8
PARAMS = pltpu.CompilerParams(vmem_limit_bytes=40 * 1024 * 1024)
NN = (((1,), (0,)), ((), ()))
NT = (((1,), (1,)), ((), ()))


def split(x):
    high = x.astype(BF16)
    return high, (x - high.astype(F32)).astype(BF16)


def dot(a, b):
    return lax.dot_general(a, b, NN, preferred_element_type=F32)


def half_product(a, b):
    return dot(jnp.concatenate(a, axis=1), jnp.concatenate([b[0], b[0]], axis=0)) + dot(a[0], b[1])


def product(a, b, dims):
    one = functools.partial(lax.dot_general, dimension_numbers=dims, preferred_element_type=F32)
    return one(a[0], b[0]) + (one(a[0], b[1]) + one(a[1], b[0]))


def live_mask(sizes_ref, sector, first, rows, cols):
    row = lax.broadcasted_iota(jnp.int32, (rows, cols), 0) + first
    col = lax.broadcasted_iota(jnp.int32, (rows, cols), 1)
    return ((row < sizes_ref[sector, 0]) & (col < sizes_ref[sector, 1])).astype(F32)


def total(x):
    return jnp.sum(x, keepdims=True)


def halves_of(half):
    core = lax.axis_index("rep")
    mine = pl.ds(pl.multiple_of(core * half, half), half)
    other = pl.ds(pl.multiple_of((1 - core) * half, half), half)
    return mine, other


def prepare_kernel(weight, sizes_ref, conn_ref, psi_hbm, diag_hbm, left_hbm, right_hbm, *refs):
    lh, ll, th, tl, rh, rl, mask_ref, own_ref, diag_ref, slot_ref, stat_ref, psi, diag, left, right, vector_sem, left_sem, right_sem = refs
    nterm = left.shape[0]
    vectors = [
        pltpu.make_async_copy(psi_hbm.at[0], psi, vector_sem.at[0]),
        pltpu.make_async_copy(diag_hbm.at[0], diag, vector_sem.at[1]),
    ]
    lefts = [pltpu.make_async_copy(left_hbm.at[i, 0], left.at[i], left_sem.at[i]) for i in range(nterm)]
    rights = [pltpu.make_async_copy(right_hbm.at[i, 0], right.at[i], right_sem.at[i]) for i in range(nterm)]
    for copy in vectors + lefts + rights:
        copy.start()
    me = lax.axis_index("sector")
    nsec, half, blk = mask_ref.shape
    first = lax.axis_index("rep") * half
    for slot in range(nsec):
        mask_ref[slot] = live_mask(sizes_ref, me ^ slot, first, half, blk)
    for term in range(nterm):
        slot_ref[term] = jnp.full(slot_ref.shape[1:], conn_ref[term] ^ me, jnp.int32)
    for copy in vectors:
        copy.wait()
    core = lax.axis_index("rep")
    mine, other = halves_of(half)
    diag_ref[:half] = diag[mine, :]
    diag_ref[half:] = diag[other, :]
    own_ref[:half] = psi[mine, :] * mask_ref[0]
    own_ref[half:] = psi[other, :] * live_mask(sizes_ref, me, (1 - core) * half, half, blk)
    square = own_ref[...] * own_ref[...]
    row = lax.broadcasted_iota(jnp.int32, stat_ref.shape, 0)
    stat_ref[...] = jnp.where(row == 0, total(square), total(square * diag_ref[...]) * weight)
    for term in range(nterm):
        lefts[term].wait()
        value = jnp.concatenate([left[term, mine, :], left[term, other, :]], axis=0)
        parts = value[:, :half], value[:, half:]
        value = jnp.concatenate([jnp.where(core == 0, *parts), jnp.where(core == 0, *parts[::-1])], axis=1)
        lh[term], ll[term] = split(value)
        th[term], tl[term] = split(value.T)
    for term in range(nterm):
        rights[term].wait()
        rh[term], rl[term] = split(right[term])


def pick(slot_ref, term, blocks):
    slot = jnp.broadcast_to(slot_ref[term, :1, :], blocks[0].shape)
    value = blocks[0]
    for index in range(1, len(blocks)):
        value = jnp.where(slot == index, blocks[index], value)
    return value


def partial_kernel(nsec, *refs):
    nears = refs[:nsec]
    slot_ref, lh, ll, part_ref = refs[nsec:]
    half = lh.shape[-1] // 2
    blocks = [near[:half] for near in nears]
    for i in range(lh.shape[0]):
        part_ref[i] = half_product((lh[i, :, :half], ll[i, :, :half]), split(pick(slot_ref, i, blocks)))


def sum_rows(coupling, first, slot_ref, th, tl, inner, joints, scalar, out_ref):
    blk = th.shape[-1]
    half = blk // 2
    rows = slice(first, first + half)
    terms = range(th.shape[0])
    returned = [product((th[i, rows, :], tl[i, rows, :]), inner[i], NN) for i in terms]
    for slot in range(out_ref.shape[0]):
        value = coupling * sum([joint[rows] for joint in joints[1:]], joints[0][rows]) if slot == 0 else jnp.zeros((half, blk), F32)
        for i in terms:
            target = jnp.broadcast_to(slot_ref[i, :1, :], (half, blk))
            value = value + jnp.where(target == slot, returned[i], 0.0)
        for tile in range(blk // LANES):
            out_ref[slot, tile * half : (tile + 1) * half, :] = value[:, tile * LANES : (tile + 1) * LANES]
        out_ref[slot, blk // LANES * half :, :] = jnp.broadcast_to(scalar, (PAD, LANES))


def keep_kernel(coupling, slot_ref, norm_ref, joint_ref, th, tl, ih, il, keep_ref):
    terms = range(th.shape[0])
    inner = [(ih[i], il[i]) for i in terms]
    sum_rows(coupling, 0, slot_ref, th, tl, inner, [joint_ref.at[i] for i in terms], norm_ref[1:2, :1], keep_ref)


def image_kernel(coupling, ncell, nsec, *refs):
    halves = refs[: 2 * (nsec - 1)]
    own_ref, part_ref, slot_ref, stat_ref = refs[2 * (nsec - 1) : 2 * (nsec - 1) + 4]
    lh, ll, th, tl, rh, rl, send_ref, full_ref, norm_ref, joint_ref, ih, il = refs[2 * (nsec - 1) + 4 :]
    blk = own_ref.shape[0]
    half = blk // 2
    nterm = lh.shape[0]
    own = own_ref[...]
    blocks = [own] + [
        jnp.concatenate([halves[2 * slot - 2][...], halves[2 * slot - 1][...]], axis=0) for slot in range(1, nsec)
    ]
    for slot in range(nsec):
        full_ref[slot] = blocks[slot]
    norm = stat_ref[:1, :1]
    for block in blocks[1:]:
        norm = norm + total(block * block)
    terms = range(nterm)
    fars = [block[half:] for block in blocks]
    middles = [
        part_ref[i] + half_product((lh[i, :, half:], ll[i, :, half:]), split(pick(slot_ref, i, fars))) for i in terms
    ]
    joints = [coupling * own + product(split(middles[i]), (rh[i], rl[i]), NT) for i in terms]
    squares = joints[0] * joints[0]
    for joint in joints[1:]:
        squares = squares + joint * joint
    for i in terms:
        joint_ref[i] = joints[i]
    scalar = stat_ref[1:2, :1] + total(squares)
    row = lax.broadcasted_iota(jnp.int32, norm_ref.shape, 0)
    norm_ref[...] = jnp.where(row == 0, norm / ncell, scalar)
    inner = [split(product(split(joints[i]), (rh[i], rl[i]), NN)) for i in terms]
    for i in terms:
        ih[i], il[i] = inner[i]
    sum_rows(coupling, half, slot_ref, th, tl, inner, joints, scalar, send_ref)


def fresh_kernel(ncell, ntile, *refs):
    parts = refs[: 2 * ntile]
    full_ref, mask_ref, diag_ref, norm_ref, fresh_ref, cross_ref = refs[2 * ntile :]
    half = fresh_ref.shape[0]
    norm = norm_ref[:1, :1]
    scale = 1.0 / jnp.sqrt(norm)
    sums = [parts[2 * tile][...] + parts[2 * tile + 1][...] for tile in range(ntile)]
    theta = sums[-1][half : half + 1, :1] / (ncell * norm)
    summed = jnp.concatenate([tile[:half] for tile in sums], axis=1)
    trial = full_ref[0, :half] * scale
    diag = diag_ref[:half]
    image = (diag * trial + summed * scale) * mask_ref[0]
    residue = image - theta * trial
    shifted = diag - theta
    fresh = residue * shifted / (shifted * shifted + 1.0)
    fresh_ref[...] = fresh
    row = lax.broadcasted_iota(jnp.int32, cross_ref.shape, 0)
    cross_ref[...] = jnp.where(row == 0, total(residue * fresh), theta)


def corner_kernel(coupling, weight, ncell, share, nsec, *refs):
    nears, fars = refs[:nsec], refs[nsec : 2 * nsec]
    part_ref, joint_ref, full_ref, diag_ref, norm_ref, cross_ref, slot_ref, lh, ll, rh, rl = refs[2 * nsec : 2 * nsec + 11]
    sums_ref, fresh_ref, info_ref = refs[2 * nsec + 11 :]
    half = nears[0].shape[0]
    terms = range(lh.shape[0])
    blocks = [far[...] for far in fars]
    middles = [
        part_ref[i] + half_product((lh[i, :, half:], ll[i, :, half:]), split(pick(slot_ref, i, blocks))) for i in terms
    ]
    norm = norm_ref[:1, :1]
    raw = [jnp.concatenate([nears[slot][...], blocks[slot]], axis=0) for slot in range(nsec)]
    overlap = full_ref[0] * raw[0]
    for slot in range(1, nsec):
        overlap = overlap + full_ref[slot] * raw[slot]
    overlap = total(overlap) / (ncell * norm)
    fresh = [raw[slot] - overlap * full_ref[slot] for slot in range(nsec)]
    length = fresh[0] * fresh[0]
    for slot in range(1, nsec):
        length = length + fresh[slot] * fresh[slot]
    length = total(length) / ncell
    fresh_ref[...] = fresh[0]
    squares = weight * fresh[0] * fresh[0] * diag_ref[...]
    for i in terms:
        joint = coupling * raw[0] + product(split(middles[i]), (rh[i], rl[i]), NT)
        joint = joint - overlap * joint_ref[i]
        squares = squares + joint * joint
    row = lax.broadcasted_iota(jnp.int32, sums_ref.shape, 0)
    sums_ref[...] = jnp.where(row == 0, total(squares), cross_ref[:1, :1] * share)
    info_ref[...] = jnp.where(row == 0, norm, jnp.where(row == 1, length, cross_ref[1:2, :1]))


def result_kernel(ncell, sums_ref, info_ref, full_ref, fresh_ref, vector_ref, energy_ref):
    sums, info = sums_ref[...], info_ref[...]
    norm, length, theta = info[0:1, :1], info[1:2, :1], info[2:3, :1]
    corner = sums[0:1, :1] / (ncell * length)
    cross = sums[1:2, :1] / (ncell * jnp.sqrt(length))
    spread = (theta - corner) / 2.0
    lowest = (theta + corner) / 2.0 - jnp.sqrt(spread * spread + cross * cross)
    keep = corner - lowest
    turn = -cross
    size = jnp.sqrt(keep * keep + turn * turn)
    keep = keep / size
    turn = turn / size
    value = (keep / jnp.sqrt(norm)) * full_ref[0] + (turn / jnp.sqrt(length)) * fresh_ref[...]
    half = value.shape[0] // 2
    mine, other = halves_of(half)
    vector_ref[0, mine, :] = value[:half]
    vector_ref[0, other, :] = value[half:]
    energy_ref[0] = jnp.sum(lowest)


def across(x, axis, step):
    size = lax.axis_size(axis)
    return lax.ppermute(x, axis, [(i, i ^ step) for i in range(size)])


def diagonally(x, axis, step):
    size = lax.axis_size(axis)
    return lax.ppermute(x, (axis, "rep"), [(2 * i + c, 2 * (i ^ step) + 1 - c) for i in range(size) for c in range(2)])


def body(psi_start, diagonal, sector_sizes, conn, left_ops, right_ops):
    blk = psi_start.shape[-1]
    half = blk // 2
    nterm_dev = conn.shape[0]
    nsec, nz, nrep = lax.axis_size("sector"), lax.axis_size("terms"), lax.axis_size("rep")
    coupling = 1.0 / math.sqrt(nterm_dev * nz * nrep)
    weight = 1.0 / (nz * nrep)
    ncell = float(nsec * blk * blk)
    core = lax.axis_index("rep")
    psi = psi_start[0]
    vmem, smem, hbm = (pl.BlockSpec(memory_space=space) for space in (pltpu.VMEM, pltpu.SMEM, pltpu.HBM))
    shape = jax.ShapeDtypeStruct

    mine = lax.dynamic_slice_in_dim(psi, core * half, half, 0)
    halves = []
    for step in range(1, nsec):
        near = across(mine, "sector", step)
        halves.append(near)

    operator = (nterm_dev, blk, blk)
    *ops, mask, own, diag, slots, stat = pl.pallas_call(
        functools.partial(prepare_kernel, weight),
        out_shape=[shape(operator, BF16)] * 6
        + [shape((nsec, half, blk), F32), shape((blk, blk), F32), shape((blk, blk), F32), shape((nterm_dev, 8, blk), jnp.int32), shape((8, 128), F32)],
        in_specs=[smem] * 2 + [hbm] * 4,
        out_specs=[vmem] * 11,
        scratch_shapes=[
            pltpu.VMEM((blk, blk), F32),
            pltpu.VMEM((blk, blk), F32),
            pltpu.VMEM(operator, F32),
            pltpu.VMEM(operator, F32),
            pltpu.SemaphoreType.DMA((2,)),
            pltpu.SemaphoreType.DMA((nterm_dev,)),
            pltpu.SemaphoreType.DMA((nterm_dev,)),
        ],
        compiler_params=pltpu.CompilerParams(vmem_limit_bytes=PREPARE * 1024 * 1024),
        name="prepare",
    )(sector_sizes, conn[:, 0], psi_start, diagonal, left_ops, right_ops)
    lh, ll, th, tl, rh, rl = ops
    masked = [near * mask[slot] for slot, near in enumerate(halves, 1)]
    halves = [part for near in masked for part in (near, across(near, "rep", 1))]

    def partial(nears):
        return pl.pallas_call(
            functools.partial(partial_kernel, nsec),
            out_shape=shape(operator, F32),
            in_specs=[vmem] * (nsec + 3),
            out_specs=vmem,
            compiler_params=PARAMS,
            name="partial",
        )(*nears, slots, lh, ll)

    summed = shape((nsec, blk // LANES * half + PAD, LANES), F32)
    send, full, norm, joints, *inner = pl.pallas_call(
        functools.partial(image_kernel, coupling, ncell, nsec),
        out_shape=[
            summed,
            shape((nsec, blk, blk), F32),
            shape((8, 128), F32),
            shape(operator, F32),
            shape(operator, BF16),
            shape(operator, BF16),
        ],
        in_specs=[vmem] * (len(halves) + 10),
        out_specs=[vmem] * 6,
        compiler_params=PARAMS,
        name="image",
    )(*halves, own, partial([own, *masked]), slots, stat, lh, ll, th, tl, rh, rl)

    keep = pl.pallas_call(
        functools.partial(keep_kernel, coupling),
        out_shape=summed,
        in_specs=[vmem] * 7,
        out_specs=vmem,
        compiler_params=PARAMS,
        name="keep",
    )(slots, norm, joints, th, tl, *inner)
    chip = keep + across(send, "rep", 1)
    ntile = blk // LANES
    bounds = [tile * half for tile in range(ntile)] + [ntile * half + PAD]
    parts = []
    for tile, (low, high) in enumerate(zip(bounds[:-1], bounds[1:])):
        part = chip[0, low:high]
        for step in range(1, nsec):
            part = part + across(chip[step, low:high], "sector", step)
        steps = [1 << bit for bit in range(nz.bit_length() - 1)]
        if tile % 2:
            steps.reverse()
        for step in steps[:-1]:
            part = part + across(part, "terms", step)
        parts += [part, across(part, "terms", steps[-1])]
    fresh, cross = pl.pallas_call(
        functools.partial(fresh_kernel, ncell, ntile),
        out_shape=[shape((half, blk), F32), shape((8, 128), F32)],
        in_specs=[vmem] * (len(parts) + 4),
        out_specs=[vmem] * 2,
        compiler_params=PARAMS,
        name="fresh",
    )(*parts, full, mask, diag, norm)

    nears = [across(fresh, "sector", step) if step else fresh for step in range(nsec)]
    fars = [across(near, "rep", 1) for near in nears]
    sums, direction, info = pl.pallas_call(
        functools.partial(corner_kernel, coupling, weight, ncell, 1.0 / nz, nsec),
        out_shape=[shape((8, 128), F32), shape((blk, blk), F32), shape((8, 128), F32)],
        in_specs=[vmem] * (2 * nsec + 11),
        out_specs=[vmem] * 3,
        compiler_params=PARAMS,
        name="corner",
    )(*nears, *fars, partial(nears), joints, full, diag, norm, cross, slots, lh, ll, rh, rl)

    sums = sums + across(sums, "rep", 1)
    for axis in ("sector", "terms"):
        parts = [diagonally(sums, axis, step) for step in range(1, lax.axis_size(axis))]
        sums = functools.reduce(lambda x, y: x + y, parts, sums)
    vector, energy = pl.pallas_call(
        functools.partial(result_kernel, ncell),
        out_shape=[shape((1, blk, blk), F32), shape((1,), F32)],
        in_specs=[vmem] * 4,
        out_specs=[vmem, smem],
        compiler_params=PARAMS,
        name="result",
    )(sums, info, full, direction)
    return vector, energy


def solution(mesh):
    in_specs = (
        P(("groups", "sector"), None, None),
        P(("groups", "sector"), None, None),
        P("groups", None),
        P(("groups", "terms", "rep"), "sector"),
        P(("groups", "terms", "rep"), "sector", None, None),
        P(("groups", "terms", "rep"), "sector", None, None),
    )
    out_specs = (P(("groups", "sector"), None, None), P("groups"))
    return jax.shard_map(body, mesh=mesh, in_specs=in_specs, out_specs=out_specs, check_vma=False)
```

```python
import functools
import math

import jax
import jax.numpy as jnp
from jax import lax
from jax.experimental import pallas as pl
from jax.experimental.pallas import tpu as pltpu
from jax.sharding import PartitionSpec as P

F32 = jnp.float32
BF16 = jnp.bfloat16
PREPARE = 49
LANES = 128
PAD = 8
PARAMS = pltpu.CompilerParams(vmem_limit_bytes=40 * 1024 * 1024)
NN = (((1,), (0,)), ((), ()))
NT = (((1,), (1,)), ((), ()))


def split(x):
    high = x.astype(BF16)
    return high, (x - high.astype(F32)).astype(BF16)


def dot(a, b):
    return lax.dot_general(a, b, NN, preferred_element_type=F32)


def half_product(a, b):
    return dot(jnp.concatenate(a, axis=1), jnp.concatenate([b[0], b[0]], axis=0)) + dot(a[0], b[1])


def product(a, b, dims):
    one = functools.partial(lax.dot_general, dimension_numbers=dims, preferred_element_type=F32)
    return one(a[0], b[0]) + (one(a[0], b[1]) + one(a[1], b[0]))


def live_mask(sizes_ref, sector, first, rows, cols):
    row = lax.broadcasted_iota(jnp.int32, (rows, cols), 0) + first
    col = lax.broadcasted_iota(jnp.int32, (rows, cols), 1)
    return ((row < sizes_ref[sector, 0]) & (col < sizes_ref[sector, 1])).astype(F32)


def total(x):
    return jnp.sum(x, keepdims=True)


def halves_of(half):
    core = lax.axis_index("rep")
    mine = pl.ds(pl.multiple_of(core * half, half), half)
    other = pl.ds(pl.multiple_of((1 - core) * half, half), half)
    return mine, other


def prepare_kernel(weight, sizes_ref, conn_ref, psi_hbm, diag_hbm, left_hbm, right_hbm, *refs):
    lh, ll, th, tl, rh, rl, mask_ref, own_ref, diag_ref, slot_ref, stat_ref, psi, diag, left, right, vector_sem, left_sem, right_sem = refs
    nterm = left.shape[0]
    vectors = [
        pltpu.make_async_copy(psi_hbm.at[0], psi, vector_sem.at[0]),
        pltpu.make_async_copy(diag_hbm.at[0], diag, vector_sem.at[1]),
    ]
    lefts = [pltpu.make_async_copy(left_hbm.at[i, 0], left.at[i], left_sem.at[i]) for i in range(nterm)]
    rights = [pltpu.make_async_copy(right_hbm.at[i, 0], right.at[i], right_sem.at[i]) for i in range(nterm)]
    for copy in vectors + lefts + rights:
        copy.start()
    me = lax.axis_index("sector")
    nsec, half, blk = mask_ref.shape
    first = lax.axis_index("rep") * half
    for slot in range(nsec):
        mask_ref[slot] = live_mask(sizes_ref, me ^ slot, first, half, blk)
    for term in range(nterm):
        slot_ref[term] = jnp.full(slot_ref.shape[1:], conn_ref[term] ^ me, jnp.int32)
    for copy in vectors:
        copy.wait()
    core = lax.axis_index("rep")
    mine, other = halves_of(half)
    diag_ref[:half] = diag[mine, :]
    diag_ref[half:] = diag[other, :]
    own_ref[:half] = psi[mine, :] * mask_ref[0]
    own_ref[half:] = psi[other, :] * live_mask(sizes_ref, me, (1 - core) * half, half, blk)
    square = own_ref[...] * own_ref[...]
    row = lax.broadcasted_iota(jnp.int32, stat_ref.shape, 0)
    stat_ref[...] = jnp.where(row == 0, total(square), total(square * diag_ref[...]) * weight)
    for term in range(nterm):
        lefts[term].wait()
        value = jnp.concatenate([left[term, mine, :], left[term, other, :]], axis=0)
        parts = value[:, :half], value[:, half:]
        value = jnp.concatenate([jnp.where(core == 0, *parts), jnp.where(core == 0, *parts[::-1])], axis=1)
        lh[term], ll[term] = split(value)
        th[term], tl[term] = split(value.T)
    for term in range(nterm):
        rights[term].wait()
        rh[term], rl[term] = split(right[term])


def pick(slot_ref, term, blocks):
    slot = jnp.broadcast_to(slot_ref[term, :1, :], blocks[0].shape)
    value = blocks[0]
    for index in range(1, len(blocks)):
        value = jnp.where(slot == index, blocks[index], value)
    return value


def partial_kernel(nsec, *refs):
    nears = refs[:nsec]
    slot_ref, lh, ll, part_ref = refs[nsec:]
    half = lh.shape[-1] // 2
    blocks = [near[:half] for near in nears]
    for i in range(lh.shape[0]):
        part_ref[i] = half_product((lh[i, :, :half], ll[i, :, :half]), split(pick(slot_ref, i, blocks)))


def sum_rows(coupling, first, slot_ref, th, tl, inner, joints, scalar, out_refs):
    blk = th.shape[-1]
    half = blk // 2
    rows = slice(first, first + half)
    terms = range(th.shape[0])
    returned = [product((th[i, rows, :], tl[i, rows, :]), inner[i], NN) for i in terms]
    for slot, out_ref in enumerate(out_refs):
        value = coupling * sum([joint[rows] for joint in joints[1:]], joints[0][rows]) if slot == 0 else jnp.zeros((half, blk), F32)
        for i in terms:
            target = jnp.broadcast_to(slot_ref[i, :1, :], (half, blk))
            value = value + jnp.where(target == slot, returned[i], 0.0)
        for tile in range(blk // LANES):
            out_ref[tile * half : (tile + 1) * half, :] = value[:, tile * LANES : (tile + 1) * LANES]
        out_ref[blk // LANES * half :, :] = jnp.broadcast_to(scalar, (PAD, LANES))


def keep_kernel(coupling, slot_ref, norm_ref, joint_ref, th, tl, ih, il, *keep_refs):
    terms = range(th.shape[0])
    inner = [(ih[i], il[i]) for i in terms]
    sum_rows(coupling, 0, slot_ref, th, tl, inner, [joint_ref.at[i] for i in terms], norm_ref[1:2, :1], keep_refs)


def image_kernel(coupling, ncell, nsec, *refs):
    halves = refs[: 2 * (nsec - 1)]
    own_ref, part_ref, slot_ref, stat_ref = refs[2 * (nsec - 1) : 2 * (nsec - 1) + 4]
    lh, ll, th, tl, rh, rl, full_ref, norm_ref, joint_ref, ih, il, *send_refs = refs[2 * (nsec - 1) + 4 :]
    blk = own_ref.shape[0]
    half = blk // 2
    nterm = lh.shape[0]
    own = own_ref[...]
    blocks = [own] + [
        jnp.concatenate([halves[2 * slot - 2][...], halves[2 * slot - 1][...]], axis=0) for slot in range(1, nsec)
    ]
    for slot in range(nsec):
        full_ref[slot] = blocks[slot]
    norm = stat_ref[:1, :1]
    for block in blocks[1:]:
        norm = norm + total(block * block)
    terms = range(nterm)
    fars = [block[half:] for block in blocks]
    middles = [
        part_ref[i] + half_product((lh[i, :, half:], ll[i, :, half:]), split(pick(slot_ref, i, fars))) for i in terms
    ]
    base = coupling * own
    joints = [base + product(split(middles[i]), (rh[i], rl[i]), NT) for i in terms]
    squares = joints[0] * joints[0]
    for joint in joints[1:]:
        squares = squares + joint * joint
    for i in terms:
        joint_ref[i] = joints[i]
    scalar = stat_ref[1:2, :1] + total(squares)
    row = lax.broadcasted_iota(jnp.int32, norm_ref.shape, 0)
    norm_ref[...] = jnp.where(row == 0, norm / ncell, scalar)
    inner = [split(product(split(joints[i]), (rh[i], rl[i]), NN)) for i in terms]
    for i in terms:
        ih[i], il[i] = inner[i]
    sum_rows(coupling, half, slot_ref, th, tl, inner, joints, scalar, send_refs)


def fresh_kernel(ncell, ntile, *refs):
    parts = refs[: 2 * ntile]
    full_ref, mask_ref, diag_ref, norm_ref, fresh_ref, cross_ref = refs[2 * ntile :]
    half = fresh_ref.shape[0]
    norm = norm_ref[:1, :1]
    scale = 1.0 / jnp.sqrt(norm)
    sums = [parts[2 * tile][...] + parts[2 * tile + 1][...] for tile in range(ntile)]
    theta = sums[-1][half : half + 1, :1] / (ncell * norm)
    summed = jnp.concatenate([tile[:half] for tile in sums], axis=1)
    trial = full_ref[0, :half] * scale
    diag = diag_ref[:half]
    image = (diag * trial + summed * scale) * mask_ref[0]
    residue = image - theta * trial
    shifted = diag - theta
    fresh = residue * shifted / (shifted * shifted + 1.0)
    fresh_ref[...] = fresh
    row = lax.broadcasted_iota(jnp.int32, cross_ref.shape, 0)
    cross_ref[...] = jnp.where(row == 0, total(residue * fresh), theta)


def corner_kernel(coupling, weight, ncell, share, nsec, *refs):
    nears, fars = refs[:nsec], refs[nsec : 2 * nsec]
    part_ref, joint_ref, full_ref, diag_ref, norm_ref, cross_ref, slot_ref, lh, ll, rh, rl = refs[2 * nsec : 2 * nsec + 11]
    sums_ref, fresh_ref, info_ref = refs[2 * nsec + 11 :]
    half = nears[0].shape[0]
    terms = range(lh.shape[0])
    blocks = [far[...] for far in fars]
    middles = [
        part_ref[i] + half_product((lh[i, :, half:], ll[i, :, half:]), split(pick(slot_ref, i, blocks))) for i in terms
    ]
    norm = norm_ref[:1, :1]
    raw = [jnp.concatenate([nears[slot][...], blocks[slot]], axis=0) for slot in range(nsec)]
    overlap = full_ref[0] * raw[0]
    for slot in range(1, nsec):
        overlap = overlap + full_ref[slot] * raw[slot]
    overlap = total(overlap) / (ncell * norm)
    fresh = [raw[slot] - overlap * full_ref[slot] for slot in range(nsec)]
    length = fresh[0] * fresh[0]
    for slot in range(1, nsec):
        length = length + fresh[slot] * fresh[slot]
    length = total(length) / ncell
    fresh_ref[...] = fresh[0]
    squares = weight * fresh[0] * fresh[0] * diag_ref[...]
    base = coupling * raw[0]
    for i in terms:
        joint = base + product(split(middles[i]), (rh[i], rl[i]), NT)
        joint = joint - overlap * joint_ref[i]
        squares = squares + joint * joint
    row = lax.broadcasted_iota(jnp.int32, sums_ref.shape, 0)
    sums_ref[...] = jnp.where(row == 0, total(squares), cross_ref[:1, :1] * share)
    info_ref[...] = jnp.where(row == 0, norm, jnp.where(row == 1, length, cross_ref[1:2, :1]))


def result_kernel(ncell, sums_ref, info_ref, full_ref, fresh_ref, vector_ref, energy_ref):
    sums, info = sums_ref[...], info_ref[...]
    norm, length, theta = info[0:1, :1], info[1:2, :1], info[2:3, :1]
    corner = sums[0:1, :1] / (ncell * length)
    cross = sums[1:2, :1] / (ncell * jnp.sqrt(length))
    spread = (theta - corner) / 2.0
    lowest = (theta + corner) / 2.0 - jnp.sqrt(spread * spread + cross * cross)
    keep = corner - lowest
    turn = -cross
    size = jnp.sqrt(keep * keep + turn * turn)
    keep = keep / size
    turn = turn / size
    value = (keep / jnp.sqrt(norm)) * full_ref[0] + (turn / jnp.sqrt(length)) * fresh_ref[...]
    half = value.shape[0] // 2
    mine, other = halves_of(half)
    vector_ref[0, mine, :] = value[:half]
    vector_ref[0, other, :] = value[half:]
    energy_ref[0] = jnp.sum(lowest)


def across(x, axis, step):
    size = lax.axis_size(axis)
    return lax.ppermute(x, axis, [(i, i ^ step) for i in range(size)])


def diagonally(x, axis, step):
    size = lax.axis_size(axis)
    return lax.ppermute(x, (axis, "rep"), [(2 * i + c, 2 * (i ^ step) + 1 - c) for i in range(size) for c in range(2)])


def body(psi_start, diagonal, sector_sizes, conn, left_ops, right_ops):
    blk = psi_start.shape[-1]
    half = blk // 2
    nterm_dev = conn.shape[0]
    nsec, nz, nrep = lax.axis_size("sector"), lax.axis_size("terms"), lax.axis_size("rep")
    coupling = 1.0 / math.sqrt(nterm_dev * nz * nrep)
    weight = 1.0 / (nz * nrep)
    ncell = float(nsec * blk * blk)
    core = lax.axis_index("rep")
    psi = psi_start[0]
    vmem, smem, hbm = (pl.BlockSpec(memory_space=space) for space in (pltpu.VMEM, pltpu.SMEM, pltpu.HBM))
    shape = jax.ShapeDtypeStruct

    mine = lax.dynamic_slice_in_dim(psi, core * half, half, 0)
    halves = []
    for step in range(1, nsec):
        near = across(mine, "sector", step)
        halves.append(near)

    operator = (nterm_dev, blk, blk)
    *ops, mask, own, diag, slots, stat = pl.pallas_call(
        functools.partial(prepare_kernel, weight),
        out_shape=[shape(operator, BF16)] * 6
        + [shape((nsec, half, blk), F32), shape((blk, blk), F32), shape((blk, blk), F32), shape((nterm_dev, 8, blk), jnp.int32), shape((8, 128), F32)],
        in_specs=[smem] * 2 + [hbm] * 4,
        out_specs=[vmem] * 11,
        scratch_shapes=[
            pltpu.VMEM((blk, blk), F32),
            pltpu.VMEM((blk, blk), F32),
            pltpu.VMEM(operator, F32),
            pltpu.VMEM(operator, F32),
            pltpu.SemaphoreType.DMA((2,)),
            pltpu.SemaphoreType.DMA((nterm_dev,)),
            pltpu.SemaphoreType.DMA((nterm_dev,)),
        ],
        compiler_params=pltpu.CompilerParams(vmem_limit_bytes=PREPARE * 1024 * 1024),
        name="prepare",
    )(sector_sizes, conn[:, 0], psi_start, diagonal, left_ops, right_ops)
    lh, ll, th, tl, rh, rl = ops
    masked = [near * mask[slot] for slot, near in enumerate(halves, 1)]
    halves = [part for near in masked for part in (near, across(near, "rep", 1))]

    def partial(nears):
        return pl.pallas_call(
            functools.partial(partial_kernel, nsec),
            out_shape=shape(operator, F32),
            in_specs=[vmem] * (nsec + 3),
            out_specs=vmem,
            compiler_params=PARAMS,
            name="partial",
        )(*nears, slots, lh, ll)

    summed = [shape((blk // LANES * half + PAD, LANES), F32)] * nsec
    full, norm, joints, ih, il, *sends = pl.pallas_call(
        functools.partial(image_kernel, coupling, ncell, nsec),
        out_shape=[
            shape((nsec, blk, blk), F32),
            shape((8, 128), F32),
            shape(operator, F32),
            shape(operator, BF16),
            shape(operator, BF16),
            *summed,
        ],
        in_specs=[vmem] * (len(halves) + 10),
        out_specs=[vmem] * (5 + nsec),
        compiler_params=PARAMS,
        name="image",
    )(*halves, own, partial([own, *masked]), slots, stat, lh, ll, th, tl, rh, rl)

    keeps = pl.pallas_call(
        functools.partial(keep_kernel, coupling),
        out_shape=summed,
        in_specs=[vmem] * 7,
        out_specs=[vmem] * nsec,
        compiler_params=PARAMS,
        name="keep",
    )(slots, norm, joints, th, tl, ih, il)
    chip = [keep + across(send, "rep", 1) for keep, send in zip(keeps, sends)]
    ntile = blk // LANES
    bounds = [tile * half for tile in range(ntile)] + [ntile * half + PAD]
    parts = []
    for tile, (low, high) in enumerate(zip(bounds[:-1], bounds[1:])):
        part = chip[0][low:high]
        for step in range(1, nsec):
            part = part + across(chip[step][low:high], "sector", step)
        steps = [1 << bit for bit in range(nz.bit_length() - 1)]
        if tile % 2:
            steps.reverse()
        for step in steps[:-1]:
            part = part + across(part, "terms", step)
        parts += [part, across(part, "terms", steps[-1])]
    fresh, cross = pl.pallas_call(
        functools.partial(fresh_kernel, ncell, ntile),
        out_shape=[shape((half, blk), F32), shape((8, 128), F32)],
        in_specs=[vmem] * (len(parts) + 4),
        out_specs=[vmem] * 2,
        compiler_params=PARAMS,
        name="fresh",
    )(*parts, full, mask, diag, norm)

    nears = [across(fresh, "sector", step) if step else fresh for step in range(nsec)]
    fars = [across(near, "rep", 1) for near in nears]
    sums, direction, info = pl.pallas_call(
        functools.partial(corner_kernel, coupling, weight, ncell, 1.0 / nz, nsec),
        out_shape=[shape((8, 128), F32), shape((blk, blk), F32), shape((8, 128), F32)],
        in_specs=[vmem] * (2 * nsec + 11),
        out_specs=[vmem] * 3,
        compiler_params=PARAMS,
        name="corner",
    )(*nears, *fars, partial(nears), joints, full, diag, norm, cross, slots, lh, ll, rh, rl)

    sums = sums + across(sums, "rep", 1)
    for axis in ("sector", "terms"):
        parts = [diagonally(sums, axis, step) for step in range(1, lax.axis_size(axis))]
        sums = functools.reduce(lambda x, y: x + y, parts, sums)
    vector, energy = pl.pallas_call(
        functools.partial(result_kernel, ncell),
        out_shape=[shape((1, blk, blk), F32), shape((1,), F32)],
        in_specs=[vmem] * 4,
        out_specs=[vmem, smem],
        compiler_params=PARAMS,
        name="result",
    )(sums, info, full, direction)
    return vector, energy


def solution(mesh):
    in_specs = (
        P(("groups", "sector"), None, None),
        P(("groups", "sector"), None, None),
        P("groups", None),
        P(("groups", "terms", "rep"), "sector"),
        P(("groups", "terms", "rep"), "sector", None, None),
        P(("groups", "terms", "rep"), "sector", None, None),
    )
    out_specs = (P(("groups", "sector"), None, None), P("groups"))
    return jax.shard_map(body, mesh=mesh, in_specs=in_specs, out_specs=out_specs, check_vma=False)
```

```python
import functools
import math

import jax
import jax.numpy as jnp
from jax import lax
from jax.experimental import pallas as pl
from jax.experimental.pallas import tpu as pltpu
from jax.sharding import PartitionSpec as P

F32 = jnp.float32
BF16 = jnp.bfloat16
PREPARE = 49
LANES = 128
PAD = 8
PARAMS = pltpu.CompilerParams(vmem_limit_bytes=40 * 1024 * 1024)
NN = (((1,), (0,)), ((), ()))
NT = (((1,), (1,)), ((), ()))


def split(x):
    high = x.astype(BF16)
    return high, (x - high.astype(F32)).astype(BF16)


def dot(a, b):
    return lax.dot_general(a, b, NN, preferred_element_type=F32)


def half_product(a, b):
    return dot(jnp.concatenate(a, axis=1), jnp.concatenate([b[0], b[0]], axis=0)) + dot(a[0], b[1])


def product(a, b, dims):
    one = functools.partial(lax.dot_general, dimension_numbers=dims, preferred_element_type=F32)
    rows = a[0].shape[0]
    both = one(jnp.concatenate(a, axis=0), b[0])
    return both[:rows] + (both[rows:] + one(a[0], b[1]))


def live_mask(sizes_ref, sector, first, rows, cols):
    row = lax.broadcasted_iota(jnp.int32, (rows, cols), 0) + first
    col = lax.broadcasted_iota(jnp.int32, (rows, cols), 1)
    return ((row < sizes_ref[sector, 0]) & (col < sizes_ref[sector, 1])).astype(F32)


def total(x):
    return jnp.sum(x, keepdims=True)


def halves_of(half):
    core = lax.axis_index("rep")
    mine = pl.ds(pl.multiple_of(core * half, half), half)
    other = pl.ds(pl.multiple_of((1 - core) * half, half), half)
    return mine, other


def prepare_kernel(weight, sizes_ref, conn_ref, psi_hbm, diag_hbm, left_hbm, right_hbm, *refs):
    lh, ll, th, tl, rh, rl, mask_ref, own_ref, diag_ref, slot_ref, stat_ref, psi, diag, left, right, vector_sem, left_sem, right_sem = refs
    nterm = left.shape[0]
    vectors = [
        pltpu.make_async_copy(psi_hbm.at[0], psi, vector_sem.at[0]),
        pltpu.make_async_copy(diag_hbm.at[0], diag, vector_sem.at[1]),
    ]
    lefts = [pltpu.make_async_copy(left_hbm.at[i, 0], left.at[i], left_sem.at[i]) for i in range(nterm)]
    rights = [pltpu.make_async_copy(right_hbm.at[i, 0], right.at[i], right_sem.at[i]) for i in range(nterm)]
    for copy in vectors + lefts + rights:
        copy.start()
    me = lax.axis_index("sector")
    nsec, half, blk = mask_ref.shape
    first = lax.axis_index("rep") * half
    for slot in range(nsec):
        mask_ref[slot] = live_mask(sizes_ref, me ^ slot, first, half, blk)
    for term in range(nterm):
        slot_ref[term] = jnp.full(slot_ref.shape[1:], conn_ref[term] ^ me, jnp.int32)
    for copy in vectors:
        copy.wait()
    core = lax.axis_index("rep")
    mine, other = halves_of(half)
    diag_ref[:half] = diag[mine, :]
    diag_ref[half:] = diag[other, :]
    own_ref[:half] = psi[mine, :] * mask_ref[0]
    own_ref[half:] = psi[other, :] * live_mask(sizes_ref, me, (1 - core) * half, half, blk)
    square = own_ref[...] * own_ref[...]
    row = lax.broadcasted_iota(jnp.int32, stat_ref.shape, 0)
    stat_ref[...] = jnp.where(row == 0, total(square), total(square * diag_ref[...]) * weight)
    for term in range(nterm):
        lefts[term].wait()
        value = jnp.concatenate([left[term, mine, :], left[term, other, :]], axis=0)
        parts = value[:, :half], value[:, half:]
        value = jnp.concatenate([jnp.where(core == 0, *parts), jnp.where(core == 0, *parts[::-1])], axis=1)
        lh[term], ll[term] = split(value)
        th[term], tl[term] = split(value.T)
    for term in range(nterm):
        rights[term].wait()
        rh[term], rl[term] = split(right[term])


def pick(slot_ref, term, blocks):
    slot = jnp.broadcast_to(slot_ref[term, :1, :], blocks[0].shape)
    value = blocks[0]
    for index in range(1, len(blocks)):
        value = jnp.where(slot == index, blocks[index], value)
    return value


def partial_kernel(nsec, *refs):
    nears = refs[:nsec]
    slot_ref, lh, ll, part_ref = refs[nsec:]
    half = lh.shape[-1] // 2
    blocks = [near[:half] for near in nears]
    for i in range(lh.shape[0]):
        part_ref[i] = half_product((lh[i, :, :half], ll[i, :, :half]), split(pick(slot_ref, i, blocks)))


def sum_rows(coupling, first, slot_ref, th, tl, inner, joints, scalar, out_refs):
    blk = th.shape[-1]
    half = blk // 2
    rows = slice(first, first + half)
    terms = range(th.shape[0])
    returned = [product((th[i, rows, :], tl[i, rows, :]), inner[i], NN) for i in terms]
    for slot, out_ref in enumerate(out_refs):
        value = coupling * sum([joint[rows] for joint in joints[1:]], joints[0][rows]) if slot == 0 else jnp.zeros((half, blk), F32)
        for i in terms:
            target = jnp.broadcast_to(slot_ref[i, :1, :], (half, blk))
            value = value + jnp.where(target == slot, returned[i], 0.0)
        for tile in range(blk // LANES):
            out_ref[tile * half : (tile + 1) * half, :] = value[:, tile * LANES : (tile + 1) * LANES]
        out_ref[blk // LANES * half :, :] = jnp.broadcast_to(scalar, (PAD, LANES))


def keep_kernel(coupling, slot_ref, norm_ref, joint_ref, th, tl, ih, il, *keep_refs):
    terms = range(th.shape[0])
    inner = [(ih[i], il[i]) for i in terms]
    sum_rows(coupling, 0, slot_ref, th, tl, inner, [joint_ref.at[i] for i in terms], norm_ref[1:2, :1], keep_refs)


def image_kernel(coupling, ncell, nsec, *refs):
    halves = refs[: 2 * (nsec - 1)]
    own_ref, part_ref, slot_ref, stat_ref = refs[2 * (nsec - 1) : 2 * (nsec - 1) + 4]
    lh, ll, th, tl, rh, rl, full_ref, norm_ref, joint_ref, ih, il, *send_refs = refs[2 * (nsec - 1) + 4 :]
    blk = own_ref.shape[0]
    half = blk // 2
    nterm = lh.shape[0]
    own = own_ref[...]
    blocks = [own] + [
        jnp.concatenate([halves[2 * slot - 2][...], halves[2 * slot - 1][...]], axis=0) for slot in range(1, nsec)
    ]
    for slot in range(nsec):
        full_ref[slot] = blocks[slot]
    norm = stat_ref[:1, :1]
    for block in blocks[1:]:
        norm = norm + total(block * block)
    terms = range(nterm)
    fars = [block[half:] for block in blocks]
    middles = [
        part_ref[i] + half_product((lh[i, :, half:], ll[i, :, half:]), split(pick(slot_ref, i, fars))) for i in terms
    ]
    base = coupling * own
    joints = [base + product(split(middles[i]), (rh[i], rl[i]), NT) for i in terms]
    squares = joints[0] * joints[0]
    for joint in joints[1:]:
        squares = squares + joint * joint
    for i in terms:
        joint_ref[i] = joints[i]
    scalar = stat_ref[1:2, :1] + total(squares)
    row = lax.broadcasted_iota(jnp.int32, norm_ref.shape, 0)
    norm_ref[...] = jnp.where(row == 0, norm / ncell, scalar)
    inner = [split(product(split(joints[i]), (rh[i], rl[i]), NN)) for i in terms]
    for i in terms:
        ih[i], il[i] = inner[i]
    sum_rows(coupling, half, slot_ref, th, tl, inner, joints, scalar, send_refs)


def fresh_kernel(ncell, ntile, *refs):
    parts = refs[: 2 * ntile]
    full_ref, mask_ref, diag_ref, norm_ref, fresh_ref, cross_ref = refs[2 * ntile :]
    half = fresh_ref.shape[0]
    norm = norm_ref[:1, :1]
    scale = 1.0 / jnp.sqrt(norm)
    sums = [parts[2 * tile][...] + parts[2 * tile + 1][...] for tile in range(ntile)]
    theta = sums[-1][half : half + 1, :1] / (ncell * norm)
    summed = jnp.concatenate([tile[:half] for tile in sums], axis=1)
    trial = full_ref[0, :half] * scale
    diag = diag_ref[:half]
    image = (diag * trial + summed * scale) * mask_ref[0]
    residue = image - theta * trial
    shifted = diag - theta
    fresh = residue * shifted / (shifted * shifted + 1.0)
    fresh_ref[...] = fresh
    row = lax.broadcasted_iota(jnp.int32, cross_ref.shape, 0)
    cross_ref[...] = jnp.where(row == 0, total(residue * fresh), theta)


def corner_kernel(coupling, weight, ncell, share, nsec, *refs):
    nears, fars = refs[:nsec], refs[nsec : 2 * nsec]
    part_ref, joint_ref, full_ref, diag_ref, norm_ref, cross_ref, slot_ref, lh, ll, rh, rl = refs[2 * nsec : 2 * nsec + 11]
    sums_ref, fresh_ref, info_ref = refs[2 * nsec + 11 :]
    half = nears[0].shape[0]
    terms = range(lh.shape[0])
    blocks = [far[...] for far in fars]
    middles = [
        part_ref[i] + half_product((lh[i, :, half:], ll[i, :, half:]), split(pick(slot_ref, i, blocks))) for i in terms
    ]
    norm = norm_ref[:1, :1]
    raw = [jnp.concatenate([nears[slot][...], blocks[slot]], axis=0) for slot in range(nsec)]
    overlap = full_ref[0] * raw[0]
    for slot in range(1, nsec):
        overlap = overlap + full_ref[slot] * raw[slot]
    overlap = total(overlap) / (ncell * norm)
    fresh = [raw[slot] - overlap * full_ref[slot] for slot in range(nsec)]
    length = fresh[0] * fresh[0]
    for slot in range(1, nsec):
        length = length + fresh[slot] * fresh[slot]
    length = total(length) / ncell
    fresh_ref[...] = fresh[0]
    squares = weight * fresh[0] * fresh[0] * diag_ref[...]
    base = coupling * raw[0]
    for i in terms:
        joint = base + product(split(middles[i]), (rh[i], rl[i]), NT)
        joint = joint - overlap * joint_ref[i]
        squares = squares + joint * joint
    row = lax.broadcasted_iota(jnp.int32, sums_ref.shape, 0)
    sums_ref[...] = jnp.where(row == 0, total(squares), cross_ref[:1, :1] * share)
    info_ref[...] = jnp.where(row == 0, norm, jnp.where(row == 1, length, cross_ref[1:2, :1]))


def result_kernel(ncell, sums_ref, info_ref, full_ref, fresh_ref, vector_ref, energy_ref):
    sums, info = sums_ref[...], info_ref[...]
    norm, length, theta = info[0:1, :1], info[1:2, :1], info[2:3, :1]
    corner = sums[0:1, :1] / (ncell * length)
    cross = sums[1:2, :1] / (ncell * jnp.sqrt(length))
    spread = (theta - corner) / 2.0
    lowest = (theta + corner) / 2.0 - jnp.sqrt(spread * spread + cross * cross)
    keep = corner - lowest
    turn = -cross
    size = jnp.sqrt(keep * keep + turn * turn)
    keep = keep / size
    turn = turn / size
    value = (keep / jnp.sqrt(norm)) * full_ref[0] + (turn / jnp.sqrt(length)) * fresh_ref[...]
    half = value.shape[0] // 2
    mine, other = halves_of(half)
    vector_ref[0, mine, :] = value[:half]
    vector_ref[0, other, :] = value[half:]
    energy_ref[0] = jnp.sum(lowest)


def across(x, axis, step):
    size = lax.axis_size(axis)
    return lax.ppermute(x, axis, [(i, i ^ step) for i in range(size)])


def diagonally(x, axis, step):
    size = lax.axis_size(axis)
    return lax.ppermute(x, (axis, "rep"), [(2 * i + c, 2 * (i ^ step) + 1 - c) for i in range(size) for c in range(2)])


def body(psi_start, diagonal, sector_sizes, conn, left_ops, right_ops):
    blk = psi_start.shape[-1]
    half = blk // 2
    nterm_dev = conn.shape[0]
    nsec, nz, nrep = lax.axis_size("sector"), lax.axis_size("terms"), lax.axis_size("rep")
    coupling = 1.0 / math.sqrt(nterm_dev * nz * nrep)
    weight = 1.0 / (nz * nrep)
    ncell = float(nsec * blk * blk)
    core = lax.axis_index("rep")
    psi = psi_start[0]
    vmem, smem, hbm = (pl.BlockSpec(memory_space=space) for space in (pltpu.VMEM, pltpu.SMEM, pltpu.HBM))
    shape = jax.ShapeDtypeStruct

    mine = lax.dynamic_slice_in_dim(psi, core * half, half, 0)
    halves = []
    for step in range(1, nsec):
        near = across(mine, "sector", step)
        halves.append(near)

    operator = (nterm_dev, blk, blk)
    *ops, mask, own, diag, slots, stat = pl.pallas_call(
        functools.partial(prepare_kernel, weight),
        out_shape=[shape(operator, BF16)] * 6
        + [shape((nsec, half, blk), F32), shape((blk, blk), F32), shape((blk, blk), F32), shape((nterm_dev, 8, blk), jnp.int32), shape((8, 128), F32)],
        in_specs=[smem] * 2 + [hbm] * 4,
        out_specs=[vmem] * 11,
        scratch_shapes=[
            pltpu.VMEM((blk, blk), F32),
            pltpu.VMEM((blk, blk), F32),
            pltpu.VMEM(operator, F32),
            pltpu.VMEM(operator, F32),
            pltpu.SemaphoreType.DMA((2,)),
            pltpu.SemaphoreType.DMA((nterm_dev,)),
            pltpu.SemaphoreType.DMA((nterm_dev,)),
        ],
        compiler_params=pltpu.CompilerParams(vmem_limit_bytes=PREPARE * 1024 * 1024),
        name="prepare",
    )(sector_sizes, conn[:, 0], psi_start, diagonal, left_ops, right_ops)
    lh, ll, th, tl, rh, rl = ops
    masked = [near * mask[slot] for slot, near in enumerate(halves, 1)]
    halves = [part for near in masked for part in (near, across(near, "rep", 1))]

    def partial(nears):
        return pl.pallas_call(
            functools.partial(partial_kernel, nsec),
            out_shape=shape(operator, F32),
            in_specs=[vmem] * (nsec + 3),
            out_specs=vmem,
            compiler_params=PARAMS,
            name="partial",
        )(*nears, slots, lh, ll)

    summed = [shape((blk // LANES * half + PAD, LANES), F32)] * nsec
    full, norm, joints, ih, il, *sends = pl.pallas_call(
        functools.partial(image_kernel, coupling, ncell, nsec),
        out_shape=[
            shape((nsec, blk, blk), F32),
            shape((8, 128), F32),
            shape(operator, F32),
            shape(operator, BF16),
            shape(operator, BF16),
            *summed,
        ],
        in_specs=[vmem] * (len(halves) + 10),
        out_specs=[vmem] * (5 + nsec),
        compiler_params=PARAMS,
        name="image",
    )(*halves, own, partial([own, *masked]), slots, stat, lh, ll, th, tl, rh, rl)

    keeps = pl.pallas_call(
        functools.partial(keep_kernel, coupling),
        out_shape=summed,
        in_specs=[vmem] * 7,
        out_specs=[vmem] * nsec,
        compiler_params=PARAMS,
        name="keep",
    )(slots, norm, joints, th, tl, ih, il)
    chip = [keep + across(send, "rep", 1) for keep, send in zip(keeps, sends)]
    ntile = blk // LANES
    bounds = [tile * half for tile in range(ntile)] + [ntile * half + PAD]
    parts = []
    for tile, (low, high) in enumerate(zip(bounds[:-1], bounds[1:])):
        part = chip[0][low:high]
        for step in range(1, nsec):
            part = part + across(chip[step][low:high], "sector", step)
        steps = [1 << bit for bit in range(nz.bit_length() - 1)]
        if tile % 2:
            steps.reverse()
        for step in steps[:-1]:
            part = part + across(part, "terms", step)
        parts += [part, across(part, "terms", steps[-1])]
    fresh, cross = pl.pallas_call(
        functools.partial(fresh_kernel, ncell, ntile),
        out_shape=[shape((half, blk), F32), shape((8, 128), F32)],
        in_specs=[vmem] * (len(parts) + 4),
        out_specs=[vmem] * 2,
        compiler_params=PARAMS,
        name="fresh",
    )(*parts, full, mask, diag, norm)

    nears = [across(fresh, "sector", step) if step else fresh for step in range(nsec)]
    fars = [across(near, "rep", 1) for near in nears]
    sums, direction, info = pl.pallas_call(
        functools.partial(corner_kernel, coupling, weight, ncell, 1.0 / nz, nsec),
        out_shape=[shape((8, 128), F32), shape((blk, blk), F32), shape((8, 128), F32)],
        in_specs=[vmem] * (2 * nsec + 11),
        out_specs=[vmem] * 3,
        compiler_params=PARAMS,
        name="corner",
    )(*nears, *fars, partial(nears), joints, full, diag, norm, cross, slots, lh, ll, rh, rl)

    sums = sums + across(sums, "rep", 1)
    for axis in ("sector", "terms"):
        parts = [diagonally(sums, axis, step) for step in range(1, lax.axis_size(axis))]
        sums = functools.reduce(lambda x, y: x + y, parts, sums)
    vector, energy = pl.pallas_call(
        functools.partial(result_kernel, ncell),
        out_shape=[shape((1, blk, blk), F32), shape((1,), F32)],
        in_specs=[vmem] * 4,
        out_specs=[vmem, smem],
        compiler_params=PARAMS,
        name="result",
    )(sums, info, full, direction)
    return vector, energy


def solution(mesh):
    in_specs = (
        P(("groups", "sector"), None, None),
        P(("groups", "sector"), None, None),
        P("groups", None),
        P(("groups", "terms", "rep"), "sector"),
        P(("groups", "terms", "rep"), "sector", None, None),
        P(("groups", "terms", "rep"), "sector", None, None),
    )
    out_specs = (P(("groups", "sector"), None, None), P("groups"))
    return jax.shard_map(body, mesh=mesh, in_specs=in_specs, out_specs=out_specs, check_vma=False)
```

```python
import functools
import math

import jax
import jax.numpy as jnp
from jax import lax
from jax.experimental import pallas as pl
from jax.experimental.pallas import tpu as pltpu
from jax.sharding import PartitionSpec as P

F32 = jnp.float32
BF16 = jnp.bfloat16
PREPARE = 49
LANES = 128
PAD = 8
PARAMS = pltpu.CompilerParams(vmem_limit_bytes=40 * 1024 * 1024)
NN = (((1,), (0,)), ((), ()))
NT = (((1,), (1,)), ((), ()))


def split(x):
    high = x.astype(BF16)
    return high, (x - high.astype(F32)).astype(BF16)


def dot(a, b):
    return lax.dot_general(a, b, NN, preferred_element_type=F32)


def half_product(a, b):
    return dot(jnp.concatenate(a, axis=1), jnp.concatenate([b[0], b[0]], axis=0)) + dot(a[0], b[1])


def product(a, b, dims):
    one = functools.partial(lax.dot_general, dimension_numbers=dims, preferred_element_type=F32)
    rows = a[0].shape[0]
    both = one(jnp.concatenate(a, axis=0), b[0])
    return both[:rows] + (both[rows:] + one(a[0], b[1]))


def live_mask(sizes_ref, sector, first, rows, cols):
    row = lax.broadcasted_iota(jnp.int32, (rows, cols), 0) + first
    col = lax.broadcasted_iota(jnp.int32, (rows, cols), 1)
    return ((row < sizes_ref[sector, 0]) & (col < sizes_ref[sector, 1])).astype(F32)


def total(x):
    return jnp.sum(x, keepdims=True)


def halves_of(half):
    core = lax.axis_index("rep")
    mine = pl.ds(pl.multiple_of(core * half, half), half)
    other = pl.ds(pl.multiple_of((1 - core) * half, half), half)
    return mine, other


def prepare_kernel(weight, sizes_ref, conn_ref, psi_hbm, diag_hbm, left_hbm, right_hbm, *refs):
    lh, ll, th, tl, rh, rl, mask_ref, own_ref, diag_ref, slot_ref, stat_ref, psi, diag, left, right, vector_sem, left_sem, right_sem = refs
    nterm = left.shape[0]
    vectors = [
        pltpu.make_async_copy(psi_hbm.at[0], psi, vector_sem.at[0]),
        pltpu.make_async_copy(diag_hbm.at[0], diag, vector_sem.at[1]),
    ]
    lefts = [pltpu.make_async_copy(left_hbm.at[i, 0], left.at[i], left_sem.at[i]) for i in range(nterm)]
    rights = [pltpu.make_async_copy(right_hbm.at[i, 0], right.at[i], right_sem.at[i]) for i in range(nterm)]
    for copy in vectors + lefts + rights:
        copy.start()
    me = lax.axis_index("sector")
    nsec, half, blk = mask_ref.shape
    first = lax.axis_index("rep") * half
    for slot in range(nsec):
        mask_ref[slot] = live_mask(sizes_ref, me ^ slot, first, half, blk)
    for term in range(nterm):
        slot_ref[term] = jnp.full(slot_ref.shape[1:], conn_ref[term] ^ me, jnp.int32)
    for copy in vectors:
        copy.wait()
    core = lax.axis_index("rep")
    mine, other = halves_of(half)
    diag_ref[:half] = diag[mine, :]
    diag_ref[half:] = diag[other, :]
    own_ref[:half] = psi[mine, :] * mask_ref[0]
    own_ref[half:] = psi[other, :] * live_mask(sizes_ref, me, (1 - core) * half, half, blk)
    square = own_ref[...] * own_ref[...]
    row = lax.broadcasted_iota(jnp.int32, stat_ref.shape, 0)
    stat_ref[...] = jnp.where(row == 0, total(square), total(square * diag_ref[...]) * weight)
    for term in range(nterm):
        lefts[term].wait()
        value = jnp.concatenate([left[term, mine, :], left[term, other, :]], axis=0)
        parts = value[:, :half], value[:, half:]
        value = jnp.concatenate([jnp.where(core == 0, *parts), jnp.where(core == 0, *parts[::-1])], axis=1)
        lh[term], ll[term] = split(value)
        th[term], tl[term] = split(value.T)
    for term in range(nterm):
        rights[term].wait()
        rh[term], rl[term] = split(right[term])


def pick(slot_ref, term, blocks):
    slot = jnp.broadcast_to(slot_ref[term, :1, :], blocks[0].shape)
    value = blocks[0]
    for index in range(1, len(blocks)):
        value = jnp.where(slot == index, blocks[index], value)
    return value


def partial_kernel(nsec, *refs):
    nears = refs[:nsec]
    slot_ref, lh, ll, part_ref = refs[nsec:]
    half = lh.shape[-1] // 2
    blocks = [near[:half] for near in nears]
    for i in range(lh.shape[0]):
        part_ref[i] = half_product((lh[i, :, :half], ll[i, :, :half]), split(pick(slot_ref, i, blocks)))


def sum_rows(coupling, first, slot_ref, th, tl, inner, joints, scalar, out_refs):
    blk = th.shape[-1]
    half = blk // 2
    rows = slice(first, first + half)
    terms = range(th.shape[0])
    returned = [product((th[i, rows, :], tl[i, rows, :]), inner[i], NN) for i in terms]
    for slot, out_ref in enumerate(out_refs):
        value = coupling * sum([joint[rows] for joint in joints[1:]], joints[0][rows]) if slot == 0 else jnp.zeros((half, blk), F32)
        for i in terms:
            target = jnp.broadcast_to(slot_ref[i, :1, :], (half, blk))
            value = value + jnp.where(target == slot, returned[i], 0.0)
        for tile in range(blk // LANES):
            out_ref[tile * half : (tile + 1) * half, :] = value[:, tile * LANES : (tile + 1) * LANES]
        out_ref[blk // LANES * half :, :] = jnp.broadcast_to(scalar, (PAD, LANES))


def keep_kernel(coupling, slot_ref, norm_ref, joint_ref, th, tl, ih, il, *keep_refs):
    terms = range(th.shape[0])
    inner = [(ih[i], il[i]) for i in terms]
    sum_rows(coupling, 0, slot_ref, th, tl, inner, [joint_ref.at[i] for i in terms], norm_ref[1:2, :1], keep_refs)


def image_kernel(coupling, ncell, nsec, *refs):
    halves = refs[: 2 * (nsec - 1)]
    own_ref, part_ref, slot_ref, stat_ref = refs[2 * (nsec - 1) : 2 * (nsec - 1) + 4]
    lh, ll, th, tl, rh, rl, full_ref, norm_ref, joint_ref, ih, il, *send_refs = refs[2 * (nsec - 1) + 4 :]
    blk = own_ref.shape[0]
    half = blk // 2
    nterm = lh.shape[0]
    own = own_ref[...]
    blocks = [own] + [
        jnp.concatenate([halves[2 * slot - 2][...], halves[2 * slot - 1][...]], axis=0) for slot in range(1, nsec)
    ]
    for slot in range(nsec):
        full_ref[slot] = blocks[slot]
    norm = stat_ref[:1, :1]
    for block in blocks[1:]:
        norm = norm + total(block * block)
    terms = range(nterm)
    fars = [block[half:] for block in blocks]
    middles = [
        part_ref[i] + half_product((lh[i, :, half:], ll[i, :, half:]), split(pick(slot_ref, i, fars))) for i in terms
    ]
    base = coupling * own
    joints = [base + product(split(middles[i]), (rh[i], rl[i]), NT) for i in terms]
    squares = joints[0] * joints[0]
    for joint in joints[1:]:
        squares = squares + joint * joint
    for i in terms:
        joint_ref[i] = joints[i]
    scalar = stat_ref[1:2, :1] + total(squares)
    row = lax.broadcasted_iota(jnp.int32, norm_ref.shape, 0)
    norm_ref[...] = jnp.where(row == 0, norm / ncell, scalar)
    inner = [split(product(split(joints[i]), (rh[i], rl[i]), NN)) for i in terms]
    for i in terms:
        ih[i], il[i] = inner[i]
    sum_rows(coupling, half, slot_ref, th, tl, inner, joints, scalar, send_refs)


def fresh_kernel(ncell, ntile, *refs):
    parts = refs[: 2 * ntile]
    full_ref, mask_ref, diag_ref, norm_ref, fresh_ref, cross_ref = refs[2 * ntile :]
    half = fresh_ref.shape[0]
    norm = norm_ref[:1, :1]
    scale = 1.0 / jnp.sqrt(norm)
    sums = [parts[2 * tile][...] + parts[2 * tile + 1][...] for tile in range(ntile)]
    theta = sums[-1][half : half + 1, :1] / (ncell * norm)
    summed = jnp.concatenate([tile[:half] for tile in sums], axis=1)
    trial = full_ref[0, :half] * scale
    diag = diag_ref[:half]
    image = (diag * trial + summed * scale) * mask_ref[0]
    residue = image - theta * trial
    shifted = diag - theta
    fresh = residue * shifted / (shifted * shifted + 1.0)
    fresh_ref[...] = fresh
    row = lax.broadcasted_iota(jnp.int32, cross_ref.shape, 0)
    cross_ref[...] = jnp.where(row == 0, total(residue * fresh), theta)


def corner_kernel(coupling, weight, ncell, share, nsec, *refs):
    nears, fars = refs[:nsec], refs[nsec : 2 * nsec]
    part_ref, joint_ref, full_ref, diag_ref, norm_ref, cross_ref, slot_ref, lh, ll, rh, rl = refs[2 * nsec : 2 * nsec + 11]
    sums_ref, fresh_ref, info_ref = refs[2 * nsec + 11 :]
    half = nears[0].shape[0]
    terms = range(lh.shape[0])
    blocks = [far[...] for far in fars]
    middles = [
        part_ref[i] + half_product((lh[i, :, half:], ll[i, :, half:]), split(pick(slot_ref, i, blocks))) for i in terms
    ]
    norm = norm_ref[:1, :1]
    raw = [jnp.concatenate([nears[slot][...], blocks[slot]], axis=0) for slot in range(nsec)]
    overlap = full_ref[0] * raw[0]
    for slot in range(1, nsec):
        overlap = overlap + full_ref[slot] * raw[slot]
    overlap = total(overlap) / (ncell * norm)
    fresh = [raw[slot] - overlap * full_ref[slot] for slot in range(nsec)]
    length = fresh[0] * fresh[0]
    for slot in range(1, nsec):
        length = length + fresh[slot] * fresh[slot]
    length = total(length) / ncell
    fresh_ref[...] = fresh[0]
    squares = weight * fresh[0] * fresh[0] * diag_ref[...]
    base = coupling * raw[0]
    for i in terms:
        joint = base + product(split(middles[i]), (rh[i], rl[i]), NT)
        joint = joint - overlap * joint_ref[i]
        squares = squares + joint * joint
    row = lax.broadcasted_iota(jnp.int32, sums_ref.shape, 0)
    sums_ref[...] = jnp.where(row == 0, total(squares), cross_ref[:1, :1] * share)
    info_ref[...] = jnp.where(row == 0, norm, jnp.where(row == 1, length, cross_ref[1:2, :1]))


def result_kernel(ncell, *refs):
    info_ref, full_ref, fresh_ref, vector_ref, energy_ref = refs[-5:]
    info = info_ref[...]
    sums = functools.reduce(lambda x, y: x + y, [ref[...] for ref in refs[:-5]])
    norm, length, theta = info[0:1, :1], info[1:2, :1], info[2:3, :1]
    corner = sums[0:1, :1] / (ncell * length)
    cross = sums[1:2, :1] / (ncell * jnp.sqrt(length))
    spread = (theta - corner) / 2.0
    lowest = (theta + corner) / 2.0 - jnp.sqrt(spread * spread + cross * cross)
    keep = corner - lowest
    turn = -cross
    size = jnp.sqrt(keep * keep + turn * turn)
    keep = keep / size
    turn = turn / size
    value = (keep / jnp.sqrt(norm)) * full_ref[0] + (turn / jnp.sqrt(length)) * fresh_ref[...]
    half = value.shape[0] // 2
    mine, other = halves_of(half)
    vector_ref[0, mine, :] = value[:half]
    vector_ref[0, other, :] = value[half:]
    energy_ref[0] = jnp.sum(lowest)


def across(x, axis, step):
    size = lax.axis_size(axis)
    return lax.ppermute(x, axis, [(i, i ^ step) for i in range(size)])


def diagonally(x, axis, step):
    size = lax.axis_size(axis)
    return lax.ppermute(x, (axis, "rep"), [(2 * i + c, 2 * (i ^ step) + 1 - c) for i in range(size) for c in range(2)])


def body(psi_start, diagonal, sector_sizes, conn, left_ops, right_ops):
    blk = psi_start.shape[-1]
    half = blk // 2
    nterm_dev = conn.shape[0]
    nsec, nz, nrep = lax.axis_size("sector"), lax.axis_size("terms"), lax.axis_size("rep")
    coupling = 1.0 / math.sqrt(nterm_dev * nz * nrep)
    weight = 1.0 / (nz * nrep)
    ncell = float(nsec * blk * blk)
    core = lax.axis_index("rep")
    psi = psi_start[0]
    vmem, smem, hbm = (pl.BlockSpec(memory_space=space) for space in (pltpu.VMEM, pltpu.SMEM, pltpu.HBM))
    shape = jax.ShapeDtypeStruct

    mine = lax.dynamic_slice_in_dim(psi, core * half, half, 0)
    halves = []
    for step in range(1, nsec):
        near = across(mine, "sector", step)
        halves.append(near)

    operator = (nterm_dev, blk, blk)
    *ops, mask, own, diag, slots, stat = pl.pallas_call(
        functools.partial(prepare_kernel, weight),
        out_shape=[shape(operator, BF16)] * 6
        + [shape((nsec, half, blk), F32), shape((blk, blk), F32), shape((blk, blk), F32), shape((nterm_dev, 8, blk), jnp.int32), shape((8, 128), F32)],
        in_specs=[smem] * 2 + [hbm] * 4,
        out_specs=[vmem] * 11,
        scratch_shapes=[
            pltpu.VMEM((blk, blk), F32),
            pltpu.VMEM((blk, blk), F32),
            pltpu.VMEM(operator, F32),
            pltpu.VMEM(operator, F32),
            pltpu.SemaphoreType.DMA((2,)),
            pltpu.SemaphoreType.DMA((nterm_dev,)),
            pltpu.SemaphoreType.DMA((nterm_dev,)),
        ],
        compiler_params=pltpu.CompilerParams(vmem_limit_bytes=PREPARE * 1024 * 1024),
        name="prepare",
    )(sector_sizes, conn[:, 0], psi_start, diagonal, left_ops, right_ops)
    lh, ll, th, tl, rh, rl = ops
    masked = [near * mask[slot] for slot, near in enumerate(halves, 1)]
    halves = [part for near in masked for part in (near, across(near, "rep", 1))]

    def partial(nears):
        return pl.pallas_call(
            functools.partial(partial_kernel, nsec),
            out_shape=shape(operator, F32),
            in_specs=[vmem] * (nsec + 3),
            out_specs=vmem,
            compiler_params=PARAMS,
            name="partial",
        )(*nears, slots, lh, ll)

    summed = [shape((blk // LANES * half + PAD, LANES), F32)] * nsec
    full, norm, joints, ih, il, *sends = pl.pallas_call(
        functools.partial(image_kernel, coupling, ncell, nsec),
        out_shape=[
            shape((nsec, blk, blk), F32),
            shape((8, 128), F32),
            shape(operator, F32),
            shape(operator, BF16),
            shape(operator, BF16),
            *summed,
        ],
        in_specs=[vmem] * (len(halves) + 10),
        out_specs=[vmem] * (5 + nsec),
        compiler_params=PARAMS,
        name="image",
    )(*halves, own, partial([own, *masked]), slots, stat, lh, ll, th, tl, rh, rl)

    keeps = pl.pallas_call(
        functools.partial(keep_kernel, coupling),
        out_shape=summed,
        in_specs=[vmem] * 7,
        out_specs=[vmem] * nsec,
        compiler_params=PARAMS,
        name="keep",
    )(slots, norm, joints, th, tl, ih, il)
    chip = [keep + across(send, "rep", 1) for keep, send in zip(keeps, sends)]
    ntile = blk // LANES
    bounds = [tile * half for tile in range(ntile)] + [ntile * half + PAD]
    parts = []
    for tile, (low, high) in enumerate(zip(bounds[:-1], bounds[1:])):
        part = chip[0][low:high]
        for step in range(1, nsec):
            part = part + across(chip[step][low:high], "sector", step)
        steps = [1 << bit for bit in range(nz.bit_length() - 1)]
        if tile % 2:
            steps.reverse()
        for step in steps[:-1]:
            part = part + across(part, "terms", step)
        parts += [part, across(part, "terms", steps[-1])]
    fresh, cross = pl.pallas_call(
        functools.partial(fresh_kernel, ncell, ntile),
        out_shape=[shape((half, blk), F32), shape((8, 128), F32)],
        in_specs=[vmem] * (len(parts) + 4),
        out_specs=[vmem] * 2,
        compiler_params=PARAMS,
        name="fresh",
    )(*parts, full, mask, diag, norm)

    nears = [across(fresh, "sector", step) if step else fresh for step in range(nsec)]
    fars = [across(near, "rep", 1) for near in nears]
    sums, direction, info = pl.pallas_call(
        functools.partial(corner_kernel, coupling, weight, ncell, 1.0 / nz, nsec),
        out_shape=[shape((8, 128), F32), shape((blk, blk), F32), shape((8, 128), F32)],
        in_specs=[vmem] * (2 * nsec + 11),
        out_specs=[vmem] * 3,
        compiler_params=PARAMS,
        name="corner",
    )(*nears, *fars, partial(nears), joints, full, diag, norm, cross, slots, lh, ll, rh, rl)

    sums = sums + across(sums, "rep", 1)
    for axis in ("sector", "terms"):
        parts = [diagonally(sums, axis, step) for step in range(1, lax.axis_size(axis))]
        if axis == "sector":
            sums = functools.reduce(lambda x, y: x + y, parts, sums)
    vector, energy = pl.pallas_call(
        functools.partial(result_kernel, ncell),
        out_shape=[shape((1, blk, blk), F32), shape((1,), F32)],
        in_specs=[vmem] * (len(parts) + 4),
        out_specs=[vmem, smem],
        compiler_params=PARAMS,
        name="result",
    )(sums, *parts, info, full, direction)
    return vector, energy


def solution(mesh):
    in_specs = (
        P(("groups", "sector"), None, None),
        P(("groups", "sector"), None, None),
        P("groups", None),
        P(("groups", "terms", "rep"), "sector"),
        P(("groups", "terms", "rep"), "sector", None, None),
        P(("groups", "terms", "rep"), "sector", None, None),
    )
    out_specs = (P(("groups", "sector"), None, None), P("groups"))
    return jax.shard_map(body, mesh=mesh, in_specs=in_specs, out_specs=out_specs, check_vma=False)
```

```python
import functools
import math

import jax
import jax.numpy as jnp
from jax import lax
from jax.experimental import pallas as pl
from jax.experimental.pallas import tpu as pltpu
from jax.sharding import PartitionSpec as P

F32 = jnp.float32
BF16 = jnp.bfloat16
PREPARE = 49
LANES = 128
PAD = 8
PARAMS = pltpu.CompilerParams(vmem_limit_bytes=40 * 1024 * 1024)
NN = (((1,), (0,)), ((), ()))
NT = (((1,), (1,)), ((), ()))


def split(x):
    high = x.astype(BF16)
    return high, (x - high.astype(F32)).astype(BF16)


def dot(a, b):
    return lax.dot_general(a, b, NN, preferred_element_type=F32)


def half_product(a, b):
    return dot(jnp.concatenate(a, axis=1), jnp.concatenate([b[0], b[0]], axis=0)) + dot(a[0], b[1])


def product(a, b, dims):
    one = functools.partial(lax.dot_general, dimension_numbers=dims, preferred_element_type=F32)
    rows = a[0].shape[0]
    both = one(jnp.concatenate(a, axis=0), b[0])
    return both[:rows] + (both[rows:] + one(a[0], b[1]))


def live_mask(sizes_ref, sector, first, rows, cols):
    row = lax.broadcasted_iota(jnp.int32, (rows, cols), 0) + first
    col = lax.broadcasted_iota(jnp.int32, (rows, cols), 1)
    return ((row < sizes_ref[sector, 0]) & (col < sizes_ref[sector, 1])).astype(F32)


def total(x):
    return jnp.sum(x, keepdims=True)


def halves_of(half):
    core = lax.axis_index("rep")
    mine = pl.ds(pl.multiple_of(core * half, half), half)
    other = pl.ds(pl.multiple_of((1 - core) * half, half), half)
    return mine, other


def prepare_kernel(weight, sizes_ref, conn_ref, psi_hbm, diag_hbm, left_hbm, right_hbm, *refs):
    lh, ll, th, tl, rh, rl, mask_ref, own_ref, diag_ref, slot_ref, stat_ref, psi, diag, left, right, vector_sem, left_sem, right_sem = refs
    nterm = left.shape[0]
    vectors = [
        pltpu.make_async_copy(psi_hbm.at[0], psi, vector_sem.at[0]),
        pltpu.make_async_copy(diag_hbm.at[0], diag, vector_sem.at[1]),
    ]
    lefts = [pltpu.make_async_copy(left_hbm.at[i, 0], left.at[i], left_sem.at[i]) for i in range(nterm)]
    rights = [pltpu.make_async_copy(right_hbm.at[i, 0], right.at[i], right_sem.at[i]) for i in range(nterm)]
    for copy in vectors + lefts + rights:
        copy.start()
    me = lax.axis_index("sector")
    nsec, half, blk = mask_ref.shape
    first = lax.axis_index("rep") * half
    for slot in range(nsec):
        mask_ref[slot] = live_mask(sizes_ref, me ^ slot, first, half, blk)
    for term in range(nterm):
        slot_ref[term] = jnp.full(slot_ref.shape[1:], conn_ref[term] ^ me, jnp.int32)
    for copy in vectors:
        copy.wait()
    core = lax.axis_index("rep")
    mine, other = halves_of(half)
    diag_ref[:half] = diag[mine, :]
    diag_ref[half:] = diag[other, :]
    own_ref[:half] = psi[mine, :] * mask_ref[0]
    own_ref[half:] = psi[other, :] * live_mask(sizes_ref, me, (1 - core) * half, half, blk)
    square = own_ref[...] * own_ref[...]
    row = lax.broadcasted_iota(jnp.int32, stat_ref.shape, 0)
    stat_ref[...] = jnp.where(row == 0, total(square), total(square * diag_ref[...]) * weight)
    for term in range(nterm):
        lefts[term].wait()
        value = jnp.concatenate([left[term, mine, :], left[term, other, :]], axis=0)
        parts = value[:, :half], value[:, half:]
        value = jnp.concatenate([jnp.where(core == 0, *parts), jnp.where(core == 0, *parts[::-1])], axis=1)
        lh[term], ll[term] = split(value)
        th[term], tl[term] = split(value.T)
    for term in range(nterm):
        rights[term].wait()
        rh[term], rl[term] = split(right[term])


def pick(slot_ref, term, blocks):
    slot = jnp.broadcast_to(slot_ref[term, :1, :], blocks[0].shape)
    value = blocks[0]
    for index in range(1, len(blocks)):
        value = jnp.where(slot == index, blocks[index], value)
    return value


def partial_kernel(nsec, *refs):
    nears = refs[:nsec]
    slot_ref, lh, ll, part_ref = refs[nsec:]
    half = lh.shape[-1] // 2
    blocks = [near[:half] for near in nears]
    for i in range(lh.shape[0]):
        part_ref[i] = half_product((lh[i, :, :half], ll[i, :, :half]), split(pick(slot_ref, i, blocks)))


def sum_rows(coupling, first, slot_ref, th, tl, inner, joints, scalar, out_refs):
    blk = th.shape[-1]
    half = blk // 2
    rows = slice(first, first + half)
    terms = range(th.shape[0])
    returned = [product((th[i, rows, :], tl[i, rows, :]), inner[i], NN) for i in terms]
    for slot, out_ref in enumerate(out_refs):
        value = coupling * sum([joint[rows] for joint in joints[1:]], joints[0][rows]) if slot == 0 else jnp.zeros((half, blk), F32)
        for i in terms:
            target = jnp.broadcast_to(slot_ref[i, :1, :], (half, blk))
            value = value + jnp.where(target == slot, returned[i], 0.0)
        for tile in range(blk // LANES):
            out_ref[tile * half : (tile + 1) * half, :] = value[:, tile * LANES : (tile + 1) * LANES]
        out_ref[blk // LANES * half :, :] = jnp.broadcast_to(scalar, (PAD, LANES))


def keep_kernel(coupling, ncell, nsec, *refs):
    halves = refs[: 2 * (nsec - 1)]
    own_ref, stat_ref, slot_ref, scalar_ref, joint_ref, th, tl, ih, il, full_ref, norm_ref, *keep_refs = refs[2 * (nsec - 1) :]
    half = own_ref.shape[0] // 2
    terms = range(th.shape[0])
    norm = stat_ref[:1, :1]
    full_ref[0] = own_ref[...]
    for slot in range(1, nsec):
        for index, part in enumerate(halves[2 * slot - 2 : 2 * slot]):
            value = part[...]
            full_ref[slot, index * half : (index + 1) * half, :] = value
            norm = norm + total(value * value)
    norm_ref[...] = jnp.broadcast_to(norm / ncell, norm_ref.shape)
    inner = [(ih[i], il[i]) for i in terms]
    sum_rows(coupling, 0, slot_ref, th, tl, inner, [joint_ref.at[i] for i in terms], scalar_ref[:1, :1], keep_refs)


def image_kernel(coupling, nsec, *refs):
    halves = refs[: 2 * (nsec - 1)]
    own_ref, part_ref, slot_ref, stat_ref = refs[2 * (nsec - 1) : 2 * (nsec - 1) + 4]
    lh, ll, th, tl, rh, rl, scalar_ref, joint_ref, ih, il, *send_refs = refs[2 * (nsec - 1) + 4 :]
    blk = own_ref.shape[0]
    half = blk // 2
    nterm = lh.shape[0]
    own = own_ref[...]
    fars = [own[half:]] + [halves[2 * slot - 1][...] for slot in range(1, nsec)]
    terms = range(nterm)
    middles = [
        part_ref[i] + half_product((lh[i, :, half:], ll[i, :, half:]), split(pick(slot_ref, i, fars))) for i in terms
    ]
    base = coupling * own
    joints = [base + product(split(middles[i]), (rh[i], rl[i]), NT) for i in terms]
    squares = joints[0] * joints[0]
    for joint in joints[1:]:
        squares = squares + joint * joint
    for i in terms:
        joint_ref[i] = joints[i]
    scalar = stat_ref[1:2, :1] + total(squares)
    scalar_ref[...] = jnp.broadcast_to(scalar, scalar_ref.shape)
    inner = [split(product(split(joints[i]), (rh[i], rl[i]), NN)) for i in terms]
    for i in terms:
        ih[i], il[i] = inner[i]
    sum_rows(coupling, half, slot_ref, th, tl, inner, joints, scalar, send_refs)


def fresh_kernel(ncell, ntile, *refs):
    parts = refs[: 2 * ntile]
    full_ref, mask_ref, diag_ref, norm_ref, fresh_ref, cross_ref = refs[2 * ntile :]
    half = fresh_ref.shape[0]
    norm = norm_ref[:1, :1]
    scale = 1.0 / jnp.sqrt(norm)
    sums = [parts[2 * tile][...] + parts[2 * tile + 1][...] for tile in range(ntile)]
    theta = sums[-1][half : half + 1, :1] / (ncell * norm)
    summed = jnp.concatenate([tile[:half] for tile in sums], axis=1)
    trial = full_ref[0, :half] * scale
    diag = diag_ref[:half]
    image = (diag * trial + summed * scale) * mask_ref[0]
    residue = image - theta * trial
    shifted = diag - theta
    fresh = residue * shifted / (shifted * shifted + 1.0)
    fresh_ref[...] = fresh
    row = lax.broadcasted_iota(jnp.int32, cross_ref.shape, 0)
    cross_ref[...] = jnp.where(row == 0, total(residue * fresh), theta)


def corner_kernel(coupling, weight, ncell, share, nsec, *refs):
    nears, fars = refs[:nsec], refs[nsec : 2 * nsec]
    part_ref, joint_ref, full_ref, diag_ref, norm_ref, cross_ref, slot_ref, lh, ll, rh, rl = refs[2 * nsec : 2 * nsec + 11]
    sums_ref, overlap_ref = refs[2 * nsec + 11 :]
    half = nears[0].shape[0]
    terms = range(lh.shape[0])
    blocks = [far[...] for far in fars]
    middles = [
        part_ref[i] + half_product((lh[i, :, half:], ll[i, :, half:]), split(pick(slot_ref, i, blocks))) for i in terms
    ]
    norm = norm_ref[:1, :1]
    raw = [jnp.concatenate([nears[slot][...], blocks[slot]], axis=0) for slot in range(nsec)]
    overlap = full_ref[0] * raw[0]
    for slot in range(1, nsec):
        overlap = overlap + full_ref[slot] * raw[slot]
    overlap = total(overlap) / (ncell * norm)
    own = raw[0] - overlap * full_ref[0]
    squares = weight * own * own * diag_ref[...]
    base = coupling * raw[0]
    for i in terms:
        joint = base + product(split(middles[i]), (rh[i], rl[i]), NT)
        joint = joint - overlap * joint_ref[i]
        squares = squares + joint * joint
    row = lax.broadcasted_iota(jnp.int32, sums_ref.shape, 0)
    sums_ref[...] = jnp.where(row == 0, total(squares), cross_ref[:1, :1] * share)
    overlap_ref[...] = jnp.broadcast_to(overlap, overlap_ref.shape)


def length_kernel(ncell, nsec, *refs):
    overlap_ref, full_ref, norm_ref, cross_ref, fresh_ref, info_ref = refs[-6:]
    half = fresh_ref.shape[0] // 2
    nears, fars = ([ref[...] for ref in part] for part in (refs[:nsec], refs[nsec : 2 * nsec]))
    overlap = overlap_ref[:1, :1]
    length = jnp.zeros((1, 1), F32)
    for slot in range(nsec):
        value = jnp.concatenate([nears[slot], fars[slot]], axis=0) - overlap * full_ref[slot]
        length = length + total(value * value)
        if slot == 0:
            fresh_ref[...] = value
    row = lax.broadcasted_iota(jnp.int32, info_ref.shape, 0)
    length = length / ncell
    info_ref[...] = jnp.where(row == 0, norm_ref[:1, :1], jnp.where(row == 1, length, cross_ref[1:2, :1]))


def result_kernel(ncell, *refs):
    info_ref, full_ref, fresh_ref, vector_ref, energy_ref = refs[-5:]
    info = info_ref[...]
    sums = functools.reduce(lambda x, y: x + y, [ref[...] for ref in refs[:-5]])
    norm, length, theta = info[0:1, :1], info[1:2, :1], info[2:3, :1]
    corner = sums[0:1, :1] / (ncell * length)
    cross = sums[1:2, :1] / (ncell * jnp.sqrt(length))
    spread = (theta - corner) / 2.0
    lowest = (theta + corner) / 2.0 - jnp.sqrt(spread * spread + cross * cross)
    keep = corner - lowest
    turn = -cross
    size = jnp.sqrt(keep * keep + turn * turn)
    keep = keep / size
    turn = turn / size
    value = (keep / jnp.sqrt(norm)) * full_ref[0] + (turn / jnp.sqrt(length)) * fresh_ref[...]
    half = value.shape[0] // 2
    mine, other = halves_of(half)
    vector_ref[0, mine, :] = value[:half]
    vector_ref[0, other, :] = value[half:]
    energy_ref[0] = jnp.sum(lowest)


def across(x, axis, step):
    size = lax.axis_size(axis)
    return lax.ppermute(x, axis, [(i, i ^ step) for i in range(size)])


def diagonally(x, axis, step):
    size = lax.axis_size(axis)
    return lax.ppermute(x, (axis, "rep"), [(2 * i + c, 2 * (i ^ step) + 1 - c) for i in range(size) for c in range(2)])


def body(psi_start, diagonal, sector_sizes, conn, left_ops, right_ops):
    blk = psi_start.shape[-1]
    half = blk // 2
    nterm_dev = conn.shape[0]
    nsec, nz, nrep = lax.axis_size("sector"), lax.axis_size("terms"), lax.axis_size("rep")
    coupling = 1.0 / math.sqrt(nterm_dev * nz * nrep)
    weight = 1.0 / (nz * nrep)
    ncell = float(nsec * blk * blk)
    core = lax.axis_index("rep")
    psi = psi_start[0]
    vmem, smem, hbm = (pl.BlockSpec(memory_space=space) for space in (pltpu.VMEM, pltpu.SMEM, pltpu.HBM))
    shape = jax.ShapeDtypeStruct

    mine = lax.dynamic_slice_in_dim(psi, core * half, half, 0)
    halves = []
    for step in range(1, nsec):
        near = across(mine, "sector", step)
        halves.append(near)

    operator = (nterm_dev, blk, blk)
    *ops, mask, own, diag, slots, stat = pl.pallas_call(
        functools.partial(prepare_kernel, weight),
        out_shape=[shape(operator, BF16)] * 6
        + [shape((nsec, half, blk), F32), shape((blk, blk), F32), shape((blk, blk), F32), shape((nterm_dev, 8, blk), jnp.int32), shape((8, 128), F32)],
        in_specs=[smem] * 2 + [hbm] * 4,
        out_specs=[vmem] * 11,
        scratch_shapes=[
            pltpu.VMEM((blk, blk), F32),
            pltpu.VMEM((blk, blk), F32),
            pltpu.VMEM(operator, F32),
            pltpu.VMEM(operator, F32),
            pltpu.SemaphoreType.DMA((2,)),
            pltpu.SemaphoreType.DMA((nterm_dev,)),
            pltpu.SemaphoreType.DMA((nterm_dev,)),
        ],
        compiler_params=pltpu.CompilerParams(vmem_limit_bytes=PREPARE * 1024 * 1024),
        name="prepare",
    )(sector_sizes, conn[:, 0], psi_start, diagonal, left_ops, right_ops)
    lh, ll, th, tl, rh, rl = ops
    masked = [near * mask[slot] for slot, near in enumerate(halves, 1)]
    halves = [part for near in masked for part in (near, across(near, "rep", 1))]

    def partial(nears):
        return pl.pallas_call(
            functools.partial(partial_kernel, nsec),
            out_shape=shape(operator, F32),
            in_specs=[vmem] * (nsec + 3),
            out_specs=vmem,
            compiler_params=PARAMS,
            name="partial",
        )(*nears, slots, lh, ll)

    summed = [shape((blk // LANES * half + PAD, LANES), F32)] * nsec
    scalar, joints, ih, il, *sends = pl.pallas_call(
        functools.partial(image_kernel, coupling, nsec),
        out_shape=[
            shape((8, 128), F32),
            shape(operator, F32),
            shape(operator, BF16),
            shape(operator, BF16),
            *summed,
        ],
        in_specs=[vmem] * (len(halves) + 10),
        out_specs=[vmem] * (4 + nsec),
        compiler_params=PARAMS,
        name="image",
    )(*halves, own, partial([own, *masked]), slots, stat, lh, ll, th, tl, rh, rl)

    full, norm, *keeps = pl.pallas_call(
        functools.partial(keep_kernel, coupling, ncell, nsec),
        out_shape=[shape((nsec, blk, blk), F32), shape((8, 128), F32), *summed],
        in_specs=[vmem] * (len(halves) + 9),
        out_specs=[vmem] * (2 + nsec),
        compiler_params=PARAMS,
        name="keep",
    )(*halves, own, stat, slots, scalar, joints, th, tl, ih, il)
    chip = [keep + across(send, "rep", 1) for keep, send in zip(keeps, sends)]
    ntile = blk // LANES
    bounds = [tile * half for tile in range(ntile)] + [ntile * half + PAD]
    parts = []
    for tile, (low, high) in enumerate(zip(bounds[:-1], bounds[1:])):
        part = chip[0][low:high]
        for step in range(1, nsec):
            part = part + across(chip[step][low:high], "sector", step)
        steps = [1 << bit for bit in range(nz.bit_length() - 1)]
        if tile % 2:
            steps.reverse()
        for step in steps[:-1]:
            part = part + across(part, "terms", step)
        parts += [part, across(part, "terms", steps[-1])]
    fresh, cross = pl.pallas_call(
        functools.partial(fresh_kernel, ncell, ntile),
        out_shape=[shape((half, blk), F32), shape((8, 128), F32)],
        in_specs=[vmem] * (len(parts) + 4),
        out_specs=[vmem] * 2,
        compiler_params=PARAMS,
        name="fresh",
    )(*parts, full, mask, diag, norm)

    nears = [across(fresh, "sector", step) if step else fresh for step in range(nsec)]
    fars = [across(near, "rep", 1) for near in nears]
    sums, overlap = pl.pallas_call(
        functools.partial(corner_kernel, coupling, weight, ncell, 1.0 / nz, nsec),
        out_shape=[shape((8, 128), F32)] * 2,
        in_specs=[vmem] * (2 * nsec + 11),
        out_specs=[vmem] * 2,
        compiler_params=PARAMS,
        name="corner",
    )(*nears, *fars, partial(nears), joints, full, diag, norm, cross, slots, lh, ll, rh, rl)

    direction, info = pl.pallas_call(
        functools.partial(length_kernel, ncell, nsec),
        out_shape=[shape((blk, blk), F32), shape((8, 128), F32)],
        in_specs=[vmem] * (2 * nsec + 4),
        out_specs=[vmem] * 2,
        compiler_params=PARAMS,
        name="length",
    )(*nears, *fars, overlap, full, norm, cross)
    sums = sums + across(sums, "rep", 1)
    for axis in ("sector", "terms"):
        parts = [diagonally(sums, axis, step) for step in range(1, lax.axis_size(axis))]
        if axis == "sector":
            sums = functools.reduce(lambda x, y: x + y, parts, sums)
    vector, energy = pl.pallas_call(
        functools.partial(result_kernel, ncell),
        out_shape=[shape((1, blk, blk), F32), shape((1,), F32)],
        in_specs=[vmem] * (len(parts) + 4),
        out_specs=[vmem, smem],
        compiler_params=PARAMS,
        name="result",
    )(sums, *parts, info, full, direction)
    return vector, energy


def solution(mesh):
    in_specs = (
        P(("groups", "sector"), None, None),
        P(("groups", "sector"), None, None),
        P("groups", None),
        P(("groups", "terms", "rep"), "sector"),
        P(("groups", "terms", "rep"), "sector", None, None),
        P(("groups", "terms", "rep"), "sector", None, None),
    )
    out_specs = (P(("groups", "sector"), None, None), P("groups"))
    return jax.shard_map(body, mesh=mesh, in_specs=in_specs, out_specs=out_specs, check_vma=False)
```
